32 devices in a mesh: sect: 2 (over x), blk: 16 (over z, y, core).
Axes of the slice: x: 2, y: 2, z: 4, core: 2. Of those that a mesh axis runs over, the one named last changes fastest.
Arguments:
- bits: int32 [2, 256], P('sect', 'blk'), may hold values from 0 to 1
- labels: int32 [128], replicated, may hold values from 0 to 127, each once
- left: bfloat16 [256, 16384], P('blk')
- tensors: bfloat16 [2, 2, 128, 128, 128], P('sect', None, 'blk')
Outputs:
- prob: float32 [2, 256], P('sect', 'blk')
- logprob: float32 [2, 256], P('sect', 'blk')
The draws below stay inside these ranges and needn't reach their ends.
Inputs may be any that keep to these rules, and one draw needn't show every extreme that they name: Every charge labels exactly one block.
All inputs are finite; a program needn't handle non-finite values.
Results may differ from the reference program's by a relative error of at most 0.0003.
Values may be sent and summed in bfloat16 or wider, within the bound.
A program may use at most 64 MiB of HBM per device.

```python
import math
import jax
import jax.numpy as jnp
from jax import lax

D = 16384
BLOCK = 128
NB = 128
SAMPLES = 256
SITES = 2


def draw_left(key, part):
    key_base = jax.random.fold_in(key, 21)
    key_block = jax.random.fold_in(key, 22)
    key_rough = jax.random.fold_in(key, 23)
    shape = (SAMPLES, NB, BLOCK)
    base = jax.random.normal(key_base, shape, jnp.float32)
    block_scale = jnp.exp(jax.random.uniform(key_block, (NB,), jnp.float32, 0.0, math.log(10.0)))
    rough = jnp.exp(jax.random.uniform(key_rough, (SAMPLES, NB), jnp.float32, math.log(0.5), math.log(2.0)))
    value = base * block_scale[None, :, None] * rough[:, :, None]
    return value.reshape(SAMPLES, D).astype(jnp.bfloat16)


def draw_tensors(key, part):
    key_base = jax.random.fold_in(key, 11)
    key_scale = jax.random.fold_in(key, 12)
    shape = (SITES, 2, NB, BLOCK, BLOCK)
    base = jax.random.normal(key_base, shape, jnp.float32)
    rise = jnp.exp(math.log(3.0) * jnp.arange(NB, dtype=jnp.float32) / (NB - 1))
    spread = jnp.exp(jax.random.uniform(key_scale, (SITES, 2, NB), jnp.float32, math.log(0.5), math.log(5.0)))
    factor = rise[None, None, :] * spread / math.sqrt(BLOCK)
    return (base * factor[:, :, :, None, None]).astype(jnp.bfloat16)


def plant(result, rng, least, high):
    longest = result.shape.index(max(result.shape))
    spots = []
    for shift in (0, 1):
        where = [jax.random.randint(jax.random.fold_in(rng, axis), (), 0, length) for axis, length in enumerate(result.shape)]
        where[longest] = (where[longest] + shift) % result.shape[longest]
        spots.append(tuple(where))
    return result.at[spots[0]].set(least).at[spots[1]].set(high)


def setup_inputs(seed: int = 0) -> dict:
    streams_of = jax.random.split(jax.random.key(seed), 5)
    bits = plant(jax.random.randint(streams_of[0], (SITES, SAMPLES), 0, 2), jax.random.fold_in(streams_of[0], 1), 0, 1).astype(jnp.int32)
    labels = jax.random.permutation(streams_of[1], NB).astype(jnp.int32)
    left = draw_left(jax.random.fold_in(streams_of[4], 71), 0)
    tensors = draw_tensors(jax.random.fold_in(streams_of[4], 71), 0)
    return dict(bits=bits, labels=labels, left=left, tensors=tensors)


def charge_order(labels, left):
    index = jnp.arange(NB, dtype=jnp.int32)
    match = labels[None, :] == index[:, None]
    source = lax.optimization_barrier(jnp.sum(jnp.where(match, index[None, :], 0), axis=1)).astype(jnp.int32)
    blocks = left.reshape(SAMPLES, NB, BLOCK)
    return jnp.take(blocks, source, axis=1).reshape(SAMPLES, D)

def reference(bits, labels, left, tensors):
    state = charge_order(labels, left).astype(jnp.float32)
    total = jnp.zeros((SAMPLES,), jnp.float32)
    probs = []
    logs = []
    for site in range(SITES):
        blocks = state.reshape(SAMPLES, NB, BLOCK)
        image = jnp.einsum('nck,bckl->bncl', blocks, tensors[site].astype(jnp.float32), precision=lax.Precision.HIGHEST)
        stay = image[0]
        raised = jnp.roll(image[1], 1, axis=1)
        norm_zero = lax.optimization_barrier(jnp.sum(stay * stay, axis=(1, 2)))
        norm_one = lax.optimization_barrier(jnp.sum(raised * raised, axis=(1, 2)))
        choose = bits[site] == 1
        chosen_norm = jnp.where(choose, norm_one, norm_zero)
        prob = chosen_norm / (norm_zero + norm_one)
        total = total + jnp.log(prob)
        chosen = jnp.where(choose[:, None, None], raised, stay)
        scaled = chosen * lax.rsqrt(chosen_norm / D + 1e-06)[:, None, None]
        state = scaled.reshape(SAMPLES, D)
        probs.append(prob)
        logs.append(total)
    return (jnp.stack(probs), jnp.stack(logs))
```

```python
import functools

import jax
import jax.numpy as jnp
from jax import lax
from jax.experimental import pallas as pl
from jax.experimental.pallas import tpu as pltpu
from jax.sharding import PartitionSpec as P

MESH = pl.DeviceIdType.MESH
EPS = 1e-06


def passed_along(value, axis, steps):
    count = lax.axis_size(axis)
    first, last = (max(0, -steps), min(count, count - steps))
    return lax.ppermute(value, axis, [(source, source + steps) for source in range(first, last)])


def charge_order(labels, left, block):
    count_blocks = labels.shape[0]
    samples_here = left.shape[0]
    blocks = left.reshape(samples_here, count_blocks, block)
    index = jnp.arange(count_blocks, dtype=jnp.int32)
    pick = (labels[None, :] == index[:, None]).astype(jnp.bfloat16)
    ordered = jnp.einsum("ci,rik->rck", pick, blocks, preferred_element_type=jnp.float32)
    return ordered.astype(jnp.bfloat16)


def site_images(state, weights, block):
    count_rows = state.shape[0]
    blocks = state.reshape(count_rows, weights.shape[1], block)
    return jnp.einsum(
        "rck,bckl->brcl",
        blocks,
        weights,
        preferred_element_type=jnp.float32,
        precision=lax.Precision.HIGHEST,
    )


def run_sections(start_rows, site_bits, advance, count):
    segment = lax.axis_index("sect")
    segments = lax.axis_size("sect")
    mrows = start_rows.shape[1]

    def one_step(step, carry):
        state, total, prob_out, log_out = carry
        group = step - segment
        valid = (group >= 0) & (group < count)
        slot = jnp.clip(group, 0, count - 1)
        first = segment == 0
        start_now = lax.dynamic_index_in_dim(start_rows, slot, 0, keepdims=False)
        state = jnp.where(first, start_now, state)
        total = jnp.where(first, jnp.zeros_like(total), total)
        bit_rows = lax.dynamic_index_in_dim(site_bits, slot, 0, keepdims=False)
        prob, next_state = advance(state, bit_rows)
        total = total + jnp.log(prob)
        old_prob = lax.dynamic_index_in_dim(prob_out, slot, 0, keepdims=False)
        old_log = lax.dynamic_index_in_dim(log_out, slot, 0, keepdims=False)
        prob_out = lax.dynamic_update_index_in_dim(
            prob_out, jnp.where(valid, prob, old_prob), slot, 0
        )
        log_out = lax.dynamic_update_index_in_dim(
            log_out, jnp.where(valid, total, old_log), slot, 0
        )
        state, total = passed_along((next_state, total), "sect", 1)
        return (state, total, prob_out, log_out)

    empty = jnp.zeros((count, mrows), jnp.float32)
    init = (start_rows[0], jnp.zeros((mrows,), jnp.float32), empty, empty)
    result = lax.fori_loop(0, count + segments - 1, one_step, init)
    return (result[2], result[3])


def body_many(bits, labels, left, tensors):
    block = tensors.shape[-1]
    count_blocks = labels.shape[0]
    width = count_blocks * block
    rows = bits.shape[1]
    ordered = charge_order(labels, left, block)
    whole = lax.all_gather(tensors, "blk", axis=2, tiled=True)[0]

    def advance(state, bit_rows):
        image = site_images(state, whole, block)
        stay = image[0]
        raised = jnp.roll(image[1], 1, axis=1)
        norm_zero = jnp.sum(stay * stay, axis=(1, 2))
        norm_one = jnp.sum(raised * raised, axis=(1, 2))
        choose = bit_rows == 1
        chosen_norm = jnp.where(choose, norm_one, norm_zero)
        prob = chosen_norm / (norm_zero + norm_one)
        chosen = jnp.where(choose[:, None, None], raised, stay)
        scaled = chosen * lax.rsqrt(chosen_norm / width + EPS)[:, None, None]
        return (prob, scaled.reshape(state.shape[0], width))

    start_rows = ordered.astype(jnp.float32).reshape(1, rows, width)
    return run_sections(start_rows, bits[0].reshape(1, rows), advance, 1)


def pair_kernel(
    ranks,
    bits_ref,
    labels_ref,
    left_ref,
    tens_ref,
    prob_ref,
    log_ref,
    bits_i,
    labels_v,
    left_v,
    left_b,
    inv_v,
    inv_s,
    ordered,
    state,
    t0,
    t1,
    part,
    inbox,
    stack,
    bits_v,
    local_sem,
    tsend_sem,
    trecv_sem,
    left_sem,
    part_sem,
):
    sect = lax.axis_index("sect")
    blk = lax.axis_index("blk")
    me = sect * ranks + blk
    total = 2 * ranks
    rows = bits_ref.shape[1]
    block = tens_ref.shape[-1]
    group = tens_ref.shape[2]
    half = group // 2
    count_blocks = group * ranks
    samples = rows * ranks
    width = count_blocks * block
    part_width = half * block

    labels_copy = pltpu.make_async_copy(labels_ref, labels_v, local_sem.at[3])
    labels_copy.start()
    bits_copy = pltpu.make_async_copy(bits_ref, bits_i, local_sem.at[4])
    bits_copy.start()
    left_copy = pltpu.make_async_copy(left_ref, left_v, local_sem.at[0])
    left_copy.start()

    @pl.when(sect == 0)
    def _():
        pltpu.make_async_copy(tens_ref.at[0, :, pl.ds(0, half)], t0, local_sem.at[1]).start()

    @pl.when(sect == 1)
    def _():
        pltpu.make_async_copy(
            tens_ref.at[0, :, pl.ds(half, half)], t1.at[:, pl.ds(0, half)], local_sem.at[1]
        ).start()

    barrier = pltpu.get_barrier_semaphore()

    def greet(k, carry):
        other = lax.rem(me + k, total)
        pl.semaphore_signal(
            barrier, inc=1, device_id=(other // ranks, lax.rem(other, ranks)), device_id_type=MESH
        )
        return carry

    lax.fori_loop(1, total, greet, 0)

    labels_copy.wait()
    labels = jnp.broadcast_to(labels_v[...].reshape(1, count_blocks), (count_blocks, count_blocks))
    place = lax.broadcasted_iota(jnp.int32, (count_blocks, count_blocks), 0)
    charge = lax.broadcasted_iota(jnp.int32, (count_blocks, count_blocks), 1)
    inv_v[...] = jnp.max(jnp.where(labels.T == charge, place, 0), axis=0, keepdims=True)
    inv_copy = pltpu.make_async_copy(inv_v, inv_s, local_sem.at[2])
    inv_copy.start()
    bits_v[...] = jnp.zeros_like(bits_v)
    bits_copy.wait()
    bits_v[0:1, 0:rows] = bits_i[...].astype(jnp.float32)
    inv_copy.wait()
    left_copy.wait()
    for i in range(count_blocks):
        left_b[i] = left_v[:, i * block : (i + 1) * block]
    for b in range(ranks):
        for h in range(half):
            where = inv_s[0, group * b + half * sect + h]
            ordered[b, :, h * block : (h + 1) * block] = left_b[where]

    pl.semaphore_wait(barrier, total - 1)

    tens_to_one = pltpu.make_async_remote_copy(
        src_ref=tens_ref.at[0, :, pl.ds(half, half)],
        dst_ref=t0,
        send_sem=tsend_sem.at[0],
        recv_sem=trecv_sem.at[0],
        device_id=(1, blk),
        device_id_type=MESH,
    )
    tens_to_zero = pltpu.make_async_remote_copy(
        src_ref=tens_ref.at[0, :, pl.ds(0, half + 1)],
        dst_ref=t1,
        send_sem=tsend_sem.at[1],
        recv_sem=trecv_sem.at[1],
        device_id=(0, blk),
        device_id_type=MESH,
    )
    tens_back = pltpu.make_async_remote_copy(
        src_ref=tens_ref.at[0, :, pl.ds(0, 1)],
        dst_ref=t1.at[:, pl.ds(half, 1)],
        send_sem=tsend_sem.at[2],
        recv_sem=trecv_sem.at[2],
        device_id=(1, lax.rem(blk + ranks - 1, ranks)),
        device_id_type=MESH,
    )

    @pl.when(sect == 0)
    def _():
        tens_to_one.start()

    @pl.when(sect == 1)
    def _():
        tens_to_zero.start()
        tens_back.start()

    mine = pl.ds(pl.multiple_of(blk * rows, rows), rows)

    def send_left(k, carry):
        other = lax.rem(blk + k, ranks)
        pltpu.make_async_remote_copy(
            src_ref=ordered.at[other],
            dst_ref=state.at[mine],
            send_sem=left_sem.at[0],
            recv_sem=left_sem.at[1],
            device_id=(sect, other),
            device_id_type=MESH,
        ).start()
        return carry

    lax.fori_loop(1, ranks, send_left, 0)
    state[mine, :] = ordered[blk]

    others = state.at[pl.ds(0, (ranks - 1) * rows)]
    pltpu.make_async_copy(others, others, left_sem.at[1]).wait()

    @pl.when(sect == 0)
    def _():
        pltpu.make_async_copy(tens_ref.at[0, :, pl.ds(0, half)], t0, local_sem.at[1]).wait()

    @pl.when(sect == 1)
    def _():
        tens_to_one.wait_recv()

    stays, raiseds = [], []
    sum_stay = jnp.zeros((samples, block), jnp.float32)
    sum_raised = jnp.zeros((samples, block), jnp.float32)
    for h in range(half):
        both = jnp.concatenate([t0[0, h], t0[1, h]], axis=1)
        image = jnp.dot(
            state[:, h * block : (h + 1) * block], both, preferred_element_type=jnp.float32
        )
        stay, raised = image[:, :block], image[:, block:]
        stays.append(stay)
        raiseds.append(raised)
        sum_stay += stay * stay
        sum_raised += raised * raised
    norm_stay = jnp.sum(sum_stay, axis=1, keepdims=True)
    norm_raised = jnp.sum(sum_raised, axis=1, keepdims=True)
    scale_stay = lax.rsqrt(norm_stay / part_width + EPS)
    scale_raised = lax.rsqrt(norm_raised / part_width + EPS)

    @pl.when(sect == 0)
    def _():
        tens_to_zero.wait_recv()

    @pl.when(sect == 1)
    def _():
        pltpu.make_async_copy(
            tens_ref.at[0, :, pl.ds(half, half)], t1.at[:, pl.ds(0, half)], local_sem.at[1]
        ).wait()
        tens_back.wait_recv()

    def halves(value):
        high = value.astype(jnp.bfloat16)
        low = (value - high.astype(jnp.float32)).astype(jnp.bfloat16)
        return jnp.concatenate([high, low], axis=1)

    sums = [[jnp.zeros((samples, block), jnp.float32) for _ in range(2)] for _ in range(2)]
    for j in range(half + 1):
        both = jnp.concatenate([t1[0, j], t1[1, j]], axis=1)
        twice = jnp.concatenate([both, both], axis=0)
        for first in range(2):
            if (first == 0 and j == half) or (first == 1 and j == 0):
                continue
            value = raiseds[j - 1] * scale_raised if first else stays[j] * scale_stay
            image = jnp.dot(halves(value), twice, preferred_element_type=jnp.float32)
            for second in range(2):
                piece = image[:, second * block : (second + 1) * block]
                sums[first][second] += piece * piece
    columns = [norm_stay, norm_raised]
    for second in range(2):
        for first in range(2):
            columns.append(jnp.sum(sums[first][second], axis=1, keepdims=True))

    lane = lax.broadcasted_iota(jnp.int32, (samples, block), 1)
    row = lax.broadcasted_iota(jnp.int32, (samples, block), 0)
    spread = jnp.zeros((samples, block), jnp.float32)
    for v, column in enumerate(columns):
        spread = jnp.where(lane // rows == v, column, spread)
    spread = jnp.where(lane % rows == row % rows, spread, 0.0)
    for b in range(ranks):
        part[b] = jnp.sum(spread[b * rows : (b + 1) * rows], axis=0, keepdims=True)
    own_bits = pltpu.roll(bits_v[...], 6 * rows, 1)[0:1]
    part[blk] = part[blk] + jnp.where(sect == 0, own_bits, 0.0)

    def send_part(k, carry):
        other = lax.rem(me + k, total)
        rank = lax.rem(other, ranks)
        pltpu.make_async_remote_copy(
            src_ref=part.at[rank],
            dst_ref=inbox.at[k - 1],
            send_sem=part_sem.at[0],
            recv_sem=part_sem.at[1],
            device_id=(other // ranks, rank),
            device_id_type=MESH,
        ).start()
        return carry

    lax.fori_loop(1, total, send_part, 0)
    pltpu.make_async_copy(inbox, inbox, part_sem.at[1]).wait()
    stack[0:1, :] = part[blk]
    for k in range(total - 1):
        stack[k + 1 : k + 2, :] = inbox[k]
    all_parts = stack[...]
    sums_all = jnp.sum(all_parts, axis=0, keepdims=True)
    weight = (all_parts / part_width + EPS) / (sums_all / width + EPS)
    lane = lax.broadcasted_iota(jnp.int32, (total, block), 1)
    weight = jnp.where(
        lane < 4 * rows, pltpu.roll(weight, 2 * rows, 1), pltpu.roll(weight, 4 * rows, 1)
    )
    later = jnp.sum(all_parts * weight, axis=0, keepdims=True)

    def value(source, v):
        wide = jnp.broadcast_to(source, (8, block))
        return wide if v == 0 else pltpu.roll(wide, block - v * rows, 1)

    bit0 = value(sums_all, 6) == 1.0
    bit1 = bits_v[...] == 1.0
    zero, one = value(sums_all, 0), value(sums_all, 1)
    prob0 = jnp.where(bit0, one, zero) / (zero + one)
    zero = jnp.where(bit0, value(later, 3), value(later, 2))
    one = jnp.where(bit0, value(later, 5), value(later, 4))
    prob1 = jnp.where(bit1, one, zero) / (zero + one)
    log0 = jnp.log(prob0)
    log1 = log0 + jnp.log(prob1)
    prob_ref[...] = jnp.where(sect == 0, prob0, prob1)[0:1, 0:rows]
    log_ref[...] = jnp.where(sect == 0, log0, log1)[0:1, 0:rows]

    pltpu.make_async_copy(others, others, left_sem.at[0]).wait()
    pltpu.make_async_copy(inbox, inbox, part_sem.at[0]).wait()

    @pl.when(sect == 0)
    def _():
        tens_to_one.wait_send()

    @pl.when(sect == 1)
    def _():
        tens_to_zero.wait_send()
        tens_back.wait_send()


def body_pair(ranks, bits, labels, left, tensors):
    rows = bits.shape[1]
    count_blocks = labels.shape[0]
    block = tensors.shape[-1]
    group = tensors.shape[2]
    half = group // 2
    vmem = pl.BlockSpec(memory_space=pltpu.VMEM)
    hbm = pl.BlockSpec(memory_space=pl.ANY)
    out = jax.ShapeDtypeStruct(bits.shape, jnp.float32)
    return pl.pallas_call(
        functools.partial(pair_kernel, ranks),
        out_shape=(out, out),
        in_specs=[hbm, hbm, hbm, hbm],
        out_specs=(vmem, vmem),
        scratch_shapes=[
            pltpu.VMEM(bits.shape, jnp.int32),
            pltpu.VMEM(labels.shape, jnp.int32),
            pltpu.VMEM(left.shape, jnp.bfloat16),
            pltpu.VMEM((count_blocks, rows, block), jnp.bfloat16),
            pltpu.VMEM((1, count_blocks), jnp.int32),
            pltpu.SMEM((1, count_blocks), jnp.int32),
            pltpu.VMEM((ranks, rows, half * block), jnp.bfloat16),
            pltpu.VMEM((ranks * rows, half * block), jnp.bfloat16),
            pltpu.VMEM((2, half, block, block), jnp.bfloat16),
            pltpu.VMEM((2, half + 1, block, block), jnp.bfloat16),
            pltpu.VMEM((ranks, 1, block), jnp.float32),
            pltpu.VMEM((2 * ranks - 1, 1, block), jnp.float32),
            pltpu.VMEM((2 * ranks, block), jnp.float32),
            pltpu.VMEM((8, block), jnp.float32),
            pltpu.SemaphoreType.DMA((5,)),
            pltpu.SemaphoreType.DMA((3,)),
            pltpu.SemaphoreType.DMA((3,)),
            pltpu.SemaphoreType.DMA((2,)),
            pltpu.SemaphoreType.DMA((2,)),
        ],
        compiler_params=pltpu.CompilerParams(
            collective_id=0, has_side_effects=True, vmem_limit_bytes=60 * 1024 * 1024
        ),
        name="score_pair",
    )(bits, labels, left, tensors)


def solution(mesh):
    in_specs = (P("sect", "blk"), P(), P("blk", None), P("sect", None, "blk", None, None))
    out_specs = (P("sect", "blk"), P("sect", "blk"))
    if mesh.shape["sect"] == 2:
        body = functools.partial(body_pair, mesh.shape["blk"])
    else:
        body = body_many
    return jax.shard_map(body, mesh=mesh, in_specs=in_specs, out_specs=out_specs, check_vma=False)
```

```python
import functools

import jax
import jax.numpy as jnp
from jax import lax
from jax.experimental import pallas as pl
from jax.experimental.pallas import tpu as pltpu
from jax.sharding import PartitionSpec as P

MESH = pl.DeviceIdType.MESH
EPS = 1e-06


def passed_along(value, axis, steps):
    count = lax.axis_size(axis)
    first, last = (max(0, -steps), min(count, count - steps))
    return lax.ppermute(value, axis, [(source, source + steps) for source in range(first, last)])


def charge_order(labels, left, block):
    count_blocks = labels.shape[0]
    samples_here = left.shape[0]
    blocks = left.reshape(samples_here, count_blocks, block)
    index = jnp.arange(count_blocks, dtype=jnp.int32)
    pick = (labels[None, :] == index[:, None]).astype(jnp.bfloat16)
    ordered = jnp.einsum("ci,rik->rck", pick, blocks, preferred_element_type=jnp.float32)
    return ordered.astype(jnp.bfloat16)


def site_images(state, weights, block):
    count_rows = state.shape[0]
    blocks = state.reshape(count_rows, weights.shape[1], block)
    return jnp.einsum(
        "rck,bckl->brcl",
        blocks,
        weights,
        preferred_element_type=jnp.float32,
        precision=lax.Precision.HIGHEST,
    )


def run_sections(start_rows, site_bits, advance, count):
    segment = lax.axis_index("sect")
    segments = lax.axis_size("sect")
    mrows = start_rows.shape[1]

    def one_step(step, carry):
        state, total, prob_out, log_out = carry
        group = step - segment
        valid = (group >= 0) & (group < count)
        slot = jnp.clip(group, 0, count - 1)
        first = segment == 0
        start_now = lax.dynamic_index_in_dim(start_rows, slot, 0, keepdims=False)
        state = jnp.where(first, start_now, state)
        total = jnp.where(first, jnp.zeros_like(total), total)
        bit_rows = lax.dynamic_index_in_dim(site_bits, slot, 0, keepdims=False)
        prob, next_state = advance(state, bit_rows)
        total = total + jnp.log(prob)
        old_prob = lax.dynamic_index_in_dim(prob_out, slot, 0, keepdims=False)
        old_log = lax.dynamic_index_in_dim(log_out, slot, 0, keepdims=False)
        prob_out = lax.dynamic_update_index_in_dim(
            prob_out, jnp.where(valid, prob, old_prob), slot, 0
        )
        log_out = lax.dynamic_update_index_in_dim(
            log_out, jnp.where(valid, total, old_log), slot, 0
        )
        state, total = passed_along((next_state, total), "sect", 1)
        return (state, total, prob_out, log_out)

    empty = jnp.zeros((count, mrows), jnp.float32)
    init = (start_rows[0], jnp.zeros((mrows,), jnp.float32), empty, empty)
    result = lax.fori_loop(0, count + segments - 1, one_step, init)
    return (result[2], result[3])


def body_many(bits, labels, left, tensors):
    block = tensors.shape[-1]
    count_blocks = labels.shape[0]
    width = count_blocks * block
    rows = bits.shape[1]
    ordered = charge_order(labels, left, block)
    whole = lax.all_gather(tensors, "blk", axis=2, tiled=True)[0]

    def advance(state, bit_rows):
        image = site_images(state, whole, block)
        stay = image[0]
        raised = jnp.roll(image[1], 1, axis=1)
        norm_zero = jnp.sum(stay * stay, axis=(1, 2))
        norm_one = jnp.sum(raised * raised, axis=(1, 2))
        choose = bit_rows == 1
        chosen_norm = jnp.where(choose, norm_one, norm_zero)
        prob = chosen_norm / (norm_zero + norm_one)
        chosen = jnp.where(choose[:, None, None], raised, stay)
        scaled = chosen * lax.rsqrt(chosen_norm / width + EPS)[:, None, None]
        return (prob, scaled.reshape(state.shape[0], width))

    start_rows = ordered.astype(jnp.float32).reshape(1, rows, width)
    return run_sections(start_rows, bits[0].reshape(1, rows), advance, 1)


def pair_kernel(
    ranks,
    bits_ref,
    labels_ref,
    left_ref,
    tens_ref,
    out_ref,
    bits_i,
    labels_v,
    left_v,
    left_b,
    inv_v,
    inv_s,
    ordered,
    state,
    images,
    t0,
    t1,
    part0,
    part1,
    inbox,
    stack,
    bits_v,
    local_sem,
    t0_send,
    t0_recv,
    t1_send,
    t1_recv,
    left_sem,
    part_sem,
):
    sect = lax.axis_index("sect")
    blk = lax.axis_index("blk")
    me = sect * ranks + blk
    total = 2 * ranks
    rows = bits_ref.shape[1]
    block = tens_ref.shape[-1]
    group = tens_ref.shape[2]
    half = group // 2
    count_blocks = group * ranks
    samples = rows * ranks
    width = count_blocks * block
    part_width = half * block

    labels_copy = pltpu.make_async_copy(labels_ref, labels_v, local_sem.at[3])
    labels_copy.start()
    left_copy = pltpu.make_async_copy(left_ref, left_v, local_sem.at[0])
    left_copy.start()
    bits_copy = pltpu.make_async_copy(bits_ref, bits_i, local_sem.at[4])
    bits_copy.start()
    own_t0 = pltpu.make_async_copy(tens_ref.at[0, :, pl.ds(0, half)], t0, local_sem.at[1])
    own_t1 = pltpu.make_async_copy(
        tens_ref.at[0, :, pl.ds(half, half)], t1.at[:, pl.ds(0, half)], local_sem.at[1]
    )

    @pl.when(sect == 0)
    def _():
        own_t0.start()

    @pl.when(sect == 1)
    def _():
        own_t1.start()

    barrier = pltpu.get_barrier_semaphore()

    def greet(k, carry):
        other = lax.rem(me + k, total)
        pl.semaphore_signal(
            barrier, inc=1, device_id=(other // ranks, lax.rem(other, ranks)), device_id_type=MESH
        )
        return carry

    lax.fori_loop(1, total, greet, 0)

    labels_copy.wait()
    labels = jnp.broadcast_to(labels_v[...].reshape(1, count_blocks), (count_blocks, count_blocks))
    place = lax.broadcasted_iota(jnp.int32, (count_blocks, count_blocks), 0)
    charge = lax.broadcasted_iota(jnp.int32, (count_blocks, count_blocks), 1)
    inv_v[...] = jnp.max(jnp.where(labels.T == charge, place, 0), axis=0, keepdims=True)
    inv_copy = pltpu.make_async_copy(inv_v, inv_s, local_sem.at[2])
    inv_copy.start()
    left_copy.wait()
    for i in range(count_blocks):
        left_b[i] = left_v[:, i * block : (i + 1) * block]
    bits_v[...] = jnp.zeros_like(bits_v)
    bits_copy.wait()
    bits_v[0:1, 0:rows] = bits_i[...].astype(jnp.float32)

    pl.semaphore_wait(barrier, total - 1)

    def tens_to_one(h):
        return pltpu.make_async_remote_copy(
            src_ref=tens_ref.at[0, :, pl.ds(half + h, 1)],
            dst_ref=t0.at[:, pl.ds(h, 1)],
            send_sem=t0_send.at[h],
            recv_sem=t0_recv.at[h],
            device_id=(1, blk),
            device_id_type=MESH,
        )

    def tens_to_zero(j):
        return pltpu.make_async_remote_copy(
            src_ref=tens_ref.at[0, :, pl.ds(j, 1)],
            dst_ref=t1.at[:, pl.ds(j, 1)],
            send_sem=t1_send.at[j],
            recv_sem=t1_recv.at[j],
            device_id=(0, blk),
            device_id_type=MESH,
        )

    tens_back = pltpu.make_async_remote_copy(
        src_ref=tens_ref.at[0, :, pl.ds(0, 1)],
        dst_ref=t1.at[:, pl.ds(half, 1)],
        send_sem=t1_send.at[half + 1],
        recv_sem=t1_recv.at[half],
        device_id=(1, lax.rem(blk + ranks - 1, ranks)),
        device_id_type=MESH,
    )

    @pl.when(sect == 0)
    def _():
        for h in range(half):
            tens_to_one(h).start()

    @pl.when(sect == 1)
    def _():
        for j in range(half + 1):
            tens_to_zero(j).start()
        tens_back.start()

    inv_copy.wait()
    for b in range(ranks):
        for h in range(half):
            where = inv_s[0, group * b + half * sect + h]
            ordered[b, :, h * block : (h + 1) * block] = left_b[where]
    mine = pl.ds(pl.multiple_of(blk * rows, rows), rows)

    def send_left(k, carry):
        other = lax.rem(blk + k, ranks)
        pltpu.make_async_remote_copy(
            src_ref=ordered.at[other],
            dst_ref=state.at[mine],
            send_sem=left_sem.at[0],
            recv_sem=left_sem.at[1],
            device_id=(sect, other),
            device_id_type=MESH,
        ).start()
        return carry

    lax.fori_loop(1, ranks, send_left, 0)
    state[mine, :] = ordered[blk]

    others = state.at[pl.ds(0, (ranks - 1) * rows)]
    pltpu.make_async_copy(others, others, left_sem.at[1]).wait()

    @pl.when(sect == 0)
    def _():
        own_t0.wait()

    sum_stay = jnp.zeros((samples, block), jnp.float32)
    sum_raised = jnp.zeros((samples, block), jnp.float32)
    for h in range(half):

        @pl.when(sect == 1)
        def _():
            tens_to_one(h).wait_recv()

        both = jnp.concatenate([t0[0, h], t0[1, h]], axis=1)
        image = jnp.dot(
            state[:, h * block : (h + 1) * block], both, preferred_element_type=jnp.float32
        )
        images[h] = image
        stay, raised = image[:, :block], image[:, block:]
        sum_stay += stay * stay
        sum_raised += raised * raised
    norm_stay = jnp.sum(sum_stay, axis=1, keepdims=True)
    norm_raised = jnp.sum(sum_raised, axis=1, keepdims=True)

    lane = lax.broadcasted_iota(jnp.int32, (samples, block), 1)
    row = lax.broadcasted_iota(jnp.int32, (samples, block), 0)

    def fill(part, columns):
        spread = jnp.zeros((samples, block), jnp.float32)
        for v, column in enumerate(columns):
            spread = jnp.where(lane // rows == v, column, spread)
        spread = jnp.where(lane % rows == row % rows, spread, 0.0)
        for b in range(ranks):
            part[b] = jnp.sum(spread[b * rows : (b + 1) * rows], axis=0, keepdims=True)

    def send_part(part, target):
        def one(k, carry):
            rank = lax.rem(blk + k, ranks)
            slot = lax.rem(target * ranks + rank - me + total, total) - 1
            pltpu.make_async_remote_copy(
                src_ref=part.at[rank],
                dst_ref=inbox.at[slot],
                send_sem=part_sem.at[0],
                recv_sem=part_sem.at[1],
                device_id=(target, rank),
                device_id_type=MESH,
            ).start()
            return carry

        lax.fori_loop(jnp.where(sect == target, 1, 0), ranks, one, 0)

    fill(part0, [norm_stay, norm_raised])
    send_part(part0, 0)

    scales = [lax.rsqrt(norm_stay / part_width + EPS), lax.rsqrt(norm_raised / part_width + EPS)]

    def halves(value):
        high = value.astype(jnp.bfloat16)
        low = (value - high.astype(jnp.float32)).astype(jnp.bfloat16)
        return jnp.concatenate([high, low], axis=1)

    @pl.when(sect == 1)
    def _():
        own_t1.wait()

    sums = [[jnp.zeros((samples, block), jnp.float32) for _ in range(2)] for _ in range(2)]
    for j in range(half + 1):
        if j == half:
            tens_to_zero(j).wait_recv()
        else:

            @pl.when(sect == 0)
            def _():
                tens_to_zero(j).wait_recv()

        both = jnp.concatenate([t1[0, j], t1[1, j]], axis=1)
        twice = jnp.concatenate([both, both], axis=0)
        for first in range(2):
            source = j - first
            if source < 0 or source == half:
                continue
            value = images[source, :, first * block : (first + 1) * block] * scales[first]
            image = jnp.dot(halves(value), twice, preferred_element_type=jnp.float32)
            for second in range(2):
                piece = image[:, second * block : (second + 1) * block]
                sums[first][second] += piece * piece
    columns = [norm_stay, norm_raised]
    for second in range(2):
        for first in range(2):
            columns.append(jnp.sum(sums[first][second], axis=1, keepdims=True))
    fill(part1, columns)
    own_bits = pltpu.roll(bits_v[...], 6 * rows, 1)[0:1]
    part1[blk] = part1[blk] + jnp.where(sect == 0, own_bits, 0.0)
    send_part(part1, 1)

    pltpu.make_async_copy(inbox, inbox, part_sem.at[1]).wait()
    stack[0:1, :] = jnp.where(sect == 0, part0[blk], part1[blk])
    for k in range(total - 1):
        stack[k + 1 : k + 2, :] = inbox[k]
    all_parts = stack[...]
    sums_all = jnp.sum(all_parts, axis=0, keepdims=True)
    here = bits_v[...] == 1.0

    def value(source, v):
        wide = jnp.broadcast_to(source, (8, block))
        return wide if v == 0 else pltpu.roll(wide, block - v * rows, 1)

    norm_zero, norm_one = value(sums_all, 0), value(sums_all, 1)

    @pl.when(sect == 0)
    def _():
        prob = jnp.where(here, norm_one, norm_zero) / (norm_zero + norm_one)
        out_ref[0:1, :] = prob[0:1]
        out_ref[1:2, :] = jnp.log(prob)[0:1]

    @pl.when(sect == 1)
    def _():
        weight = (all_parts / part_width + EPS) / (sums_all / width + EPS)
        where = lax.broadcasted_iota(jnp.int32, (total, block), 1)
        weight = jnp.where(
            where < 4 * rows, pltpu.roll(weight, 2 * rows, 1), pltpu.roll(weight, 4 * rows, 1)
        )
        later = jnp.sum(all_parts * weight, axis=0, keepdims=True)
        before = value(sums_all, 6) == 1.0
        prob0 = jnp.where(before, norm_one, norm_zero) / (norm_zero + norm_one)
        zero = jnp.where(before, value(later, 3), value(later, 2))
        one = jnp.where(before, value(later, 5), value(later, 4))
        prob = jnp.where(here, one, zero) / (zero + one)
        out_ref[0:1, :] = prob[0:1]
        out_ref[1:2, :] = (jnp.log(prob0) + jnp.log(prob))[0:1]

    pltpu.make_async_copy(others, others, left_sem.at[0]).wait()
    pltpu.make_async_copy(inbox, inbox, part_sem.at[0]).wait()

    @pl.when(sect == 0)
    def _():
        for h in range(half):
            tens_to_one(h).wait_send()

    @pl.when(sect == 1)
    def _():
        for j in range(half + 1):
            tens_to_zero(j).wait_send()
        tens_back.wait_send()


def body_pair(ranks, bits, labels, left, tensors):
    rows = bits.shape[1]
    count_blocks = labels.shape[0]
    block = tensors.shape[-1]
    group = tensors.shape[2]
    half = group // 2
    vmem = pl.BlockSpec(memory_space=pltpu.VMEM)
    hbm = pl.BlockSpec(memory_space=pl.ANY)
    dma = pltpu.SemaphoreType.DMA
    scored = pl.pallas_call(
        functools.partial(pair_kernel, ranks),
        out_shape=jax.ShapeDtypeStruct((2, block), jnp.float32),
        in_specs=[hbm, hbm, hbm, hbm],
        out_specs=vmem,
        scratch_shapes=[
            pltpu.VMEM(bits.shape, jnp.int32),
            pltpu.VMEM(labels.shape, jnp.int32),
            pltpu.VMEM(left.shape, jnp.bfloat16),
            pltpu.VMEM((count_blocks, rows, block), jnp.bfloat16),
            pltpu.VMEM((1, count_blocks), jnp.int32),
            pltpu.SMEM((1, count_blocks), jnp.int32),
            pltpu.VMEM((ranks, rows, half * block), jnp.bfloat16),
            pltpu.VMEM((ranks * rows, half * block), jnp.bfloat16),
            pltpu.VMEM((half, ranks * rows, 2 * block), jnp.float32),
            pltpu.VMEM((2, half, block, block), jnp.bfloat16),
            pltpu.VMEM((2, half + 1, block, block), jnp.bfloat16),
            pltpu.VMEM((ranks, 1, block), jnp.float32),
            pltpu.VMEM((ranks, 1, block), jnp.float32),
            pltpu.VMEM((2 * ranks - 1, 1, block), jnp.float32),
            pltpu.VMEM((2 * ranks, block), jnp.float32),
            pltpu.VMEM((8, block), jnp.float32),
            dma((5,)),
            dma((half,)),
            dma((half,)),
            dma((half + 2,)),
            dma((half + 1,)),
            dma((2,)),
            dma((2,)),
        ],
        compiler_params=pltpu.CompilerParams(
            collective_id=0, has_side_effects=True, vmem_limit_bytes=60 * 1024 * 1024
        ),
        name="score_pair",
    )(bits, labels, left, tensors)
    return scored[0:1, :rows], scored[1:2, :rows]


def solution(mesh):
    in_specs = (P("sect", "blk"), P(), P("blk", None), P("sect", None, "blk", None, None))
    out_specs = (P("sect", "blk"), P("sect", "blk"))
    if mesh.shape["sect"] == 2:
        body = functools.partial(body_pair, mesh.shape["blk"])
    else:
        body = body_many
    return jax.shard_map(body, mesh=mesh, in_specs=in_specs, out_specs=out_specs, check_vma=False)
```

```python
import functools

import jax
import jax.numpy as jnp
from jax import lax
from jax.experimental import pallas as pl
from jax.experimental.pallas import tpu as pltpu
from jax.sharding import PartitionSpec as P

MESH = pl.DeviceIdType.MESH
EPS = 1e-06


def passed_along(value, axis, steps):
    count = lax.axis_size(axis)
    first, last = (max(0, -steps), min(count, count - steps))
    return lax.ppermute(value, axis, [(source, source + steps) for source in range(first, last)])


def charge_order(labels, left, block):
    count_blocks = labels.shape[0]
    samples_here = left.shape[0]
    blocks = left.reshape(samples_here, count_blocks, block)
    index = jnp.arange(count_blocks, dtype=jnp.int32)
    pick = (labels[None, :] == index[:, None]).astype(jnp.bfloat16)
    ordered = jnp.einsum("ci,rik->rck", pick, blocks, preferred_element_type=jnp.float32)
    return ordered.astype(jnp.bfloat16)


def site_images(state, weights, block):
    count_rows = state.shape[0]
    blocks = state.reshape(count_rows, weights.shape[1], block)
    return jnp.einsum(
        "rck,bckl->brcl",
        blocks,
        weights,
        preferred_element_type=jnp.float32,
        precision=lax.Precision.HIGHEST,
    )


def run_sections(start_rows, site_bits, advance, count):
    segment = lax.axis_index("sect")
    segments = lax.axis_size("sect")
    mrows = start_rows.shape[1]

    def one_step(step, carry):
        state, total, prob_out, log_out = carry
        group = step - segment
        valid = (group >= 0) & (group < count)
        slot = jnp.clip(group, 0, count - 1)
        first = segment == 0
        start_now = lax.dynamic_index_in_dim(start_rows, slot, 0, keepdims=False)
        state = jnp.where(first, start_now, state)
        total = jnp.where(first, jnp.zeros_like(total), total)
        bit_rows = lax.dynamic_index_in_dim(site_bits, slot, 0, keepdims=False)
        prob, next_state = advance(state, bit_rows)
        total = total + jnp.log(prob)
        old_prob = lax.dynamic_index_in_dim(prob_out, slot, 0, keepdims=False)
        old_log = lax.dynamic_index_in_dim(log_out, slot, 0, keepdims=False)
        prob_out = lax.dynamic_update_index_in_dim(
            prob_out, jnp.where(valid, prob, old_prob), slot, 0
        )
        log_out = lax.dynamic_update_index_in_dim(
            log_out, jnp.where(valid, total, old_log), slot, 0
        )
        state, total = passed_along((next_state, total), "sect", 1)
        return (state, total, prob_out, log_out)

    empty = jnp.zeros((count, mrows), jnp.float32)
    init = (start_rows[0], jnp.zeros((mrows,), jnp.float32), empty, empty)
    result = lax.fori_loop(0, count + segments - 1, one_step, init)
    return (result[2], result[3])


def body_many(bits, labels, left, tensors):
    block = tensors.shape[-1]
    count_blocks = labels.shape[0]
    width = count_blocks * block
    rows = bits.shape[1]
    ordered = charge_order(labels, left, block)
    whole = lax.all_gather(tensors, "blk", axis=2, tiled=True)[0]

    def advance(state, bit_rows):
        image = site_images(state, whole, block)
        stay = image[0]
        raised = jnp.roll(image[1], 1, axis=1)
        norm_zero = jnp.sum(stay * stay, axis=(1, 2))
        norm_one = jnp.sum(raised * raised, axis=(1, 2))
        choose = bit_rows == 1
        chosen_norm = jnp.where(choose, norm_one, norm_zero)
        prob = chosen_norm / (norm_zero + norm_one)
        chosen = jnp.where(choose[:, None, None], raised, stay)
        scaled = chosen * lax.rsqrt(chosen_norm / width + EPS)[:, None, None]
        return (prob, scaled.reshape(state.shape[0], width))

    start_rows = ordered.astype(jnp.float32).reshape(1, rows, width)
    return run_sections(start_rows, bits[0].reshape(1, rows), advance, 1)


def pair_kernel(
    ranks,
    bits_ref,
    labels_ref,
    left_ref,
    tens_ref,
    out_ref,
    bits_i,
    labels_v,
    left_v,
    left_b,
    inv_v,
    inv_s,
    ordered,
    state,
    images,
    t0,
    t1,
    part0,
    part1,
    inbox,
    stack,
    bits_v,
    local_sem,
    t0_send,
    t0_recv,
    t1_send,
    t1_recv,
    left_sem,
    part_sem,
):
    sect = lax.axis_index("sect")
    blk = lax.axis_index("blk")
    me = sect * ranks + blk
    total = 2 * ranks
    rows = bits_ref.shape[1]
    block = tens_ref.shape[-1]
    group = tens_ref.shape[2]
    half = group // 2
    count_blocks = group * ranks
    samples = rows * ranks
    width = count_blocks * block
    part_width = half * block

    labels_copy = pltpu.make_async_copy(labels_ref, labels_v, local_sem.at[3])
    labels_copy.start()
    left_copy = pltpu.make_async_copy(left_ref, left_v, local_sem.at[0])
    left_copy.start()
    bits_copy = pltpu.make_async_copy(bits_ref, bits_i, local_sem.at[4])
    bits_copy.start()
    own_t0 = pltpu.make_async_copy(tens_ref.at[0, :, pl.ds(0, half)], t0, local_sem.at[1])
    own_t1 = pltpu.make_async_copy(
        tens_ref.at[0, :, pl.ds(half, half)], t1.at[:, pl.ds(0, half)], local_sem.at[1]
    )

    @pl.when(sect == 0)
    def _():
        own_t0.start()

    @pl.when(sect == 1)
    def _():
        own_t1.start()

    barrier = pltpu.get_barrier_semaphore()

    def greet(k, carry):
        other = lax.rem(me + k, total)
        pl.semaphore_signal(
            barrier, inc=1, device_id=(other // ranks, lax.rem(other, ranks)), device_id_type=MESH
        )
        return carry

    lax.fori_loop(1, total, greet, 0)

    labels_copy.wait()
    labels = jnp.broadcast_to(labels_v[...].reshape(1, count_blocks), (count_blocks, count_blocks))
    place = lax.broadcasted_iota(jnp.int32, (count_blocks, count_blocks), 0)
    charge = lax.broadcasted_iota(jnp.int32, (count_blocks, count_blocks), 1)
    inv_v[...] = jnp.max(jnp.where(labels.T == charge, place, 0), axis=0, keepdims=True)
    inv_copy = pltpu.make_async_copy(inv_v, inv_s, local_sem.at[2])
    inv_copy.start()
    left_copy.wait()
    for i in range(count_blocks):
        left_b[i] = left_v[:, i * block : (i + 1) * block]
    bits_v[...] = jnp.zeros_like(bits_v)
    bits_copy.wait()
    bits_v[0:1, 0:rows] = bits_i[...].astype(jnp.float32)
    inv_copy.wait()
    for b in range(ranks):
        for h in range(half):
            where = inv_s[0, group * b + half * sect + h]
            ordered[b, :, h * block : (h + 1) * block] = left_b[where]

    pl.semaphore_wait(barrier, total - 1)

    def tens_to_one(h):
        return pltpu.make_async_remote_copy(
            src_ref=tens_ref.at[0, :, pl.ds(half + h, 1)],
            dst_ref=t0.at[:, pl.ds(h, 1)],
            send_sem=t0_send.at[h],
            recv_sem=t0_recv.at[h],
            device_id=(1, blk),
            device_id_type=MESH,
        )

    def tens_to_zero(j):
        return pltpu.make_async_remote_copy(
            src_ref=tens_ref.at[0, :, pl.ds(j, 1)],
            dst_ref=t1.at[:, pl.ds(j, 1)],
            send_sem=t1_send.at[j],
            recv_sem=t1_recv.at[j],
            device_id=(0, blk),
            device_id_type=MESH,
        )

    tens_back = pltpu.make_async_remote_copy(
        src_ref=tens_ref.at[0, :, pl.ds(0, 1)],
        dst_ref=t1.at[:, pl.ds(half, 1)],
        send_sem=t1_send.at[half + 1],
        recv_sem=t1_recv.at[half],
        device_id=(1, lax.rem(blk + ranks - 1, ranks)),
        device_id_type=MESH,
    )

    mine = pl.ds(pl.multiple_of(blk * rows, rows), rows)

    def send_left(k):
        other = lax.rem(blk + k, ranks)
        pltpu.make_async_remote_copy(
            src_ref=ordered.at[other],
            dst_ref=state.at[mine],
            send_sem=left_sem.at[0],
            recv_sem=left_sem.at[1],
            device_id=(sect, other),
            device_id_type=MESH,
        ).start()

    far_first = sorted(range(1, ranks), key=lambda k: abs(k - ranks // 2))
    for i, k in enumerate(far_first):
        send_left(k)
        if i % 2 == 1 and i // 2 < half:

            @pl.when(sect == 0)
            def _():
                tens_to_one(i // 2).start()

            @pl.when(sect == 1)
            def _():
                tens_to_zero(i // 2).start()

    @pl.when(sect == 1)
    def _():
        tens_to_zero(half).start()
        tens_back.start()

    state[mine, :] = ordered[blk]

    others = state.at[pl.ds(0, (ranks - 1) * rows)]
    pltpu.make_async_copy(others, others, left_sem.at[1]).wait()

    @pl.when(sect == 0)
    def _():
        own_t0.wait()

    sum_stay = jnp.zeros((samples, block), jnp.float32)
    sum_raised = jnp.zeros((samples, block), jnp.float32)
    for h in range(half):

        @pl.when(sect == 1)
        def _():
            tens_to_one(h).wait_recv()

        both = jnp.concatenate([t0[0, h], t0[1, h]], axis=1)
        image = jnp.dot(
            state[:, h * block : (h + 1) * block], both, preferred_element_type=jnp.float32
        )
        images[h] = image
        stay, raised = image[:, :block], image[:, block:]
        sum_stay += stay * stay
        sum_raised += raised * raised
    norm_stay = jnp.sum(sum_stay, axis=1, keepdims=True)
    norm_raised = jnp.sum(sum_raised, axis=1, keepdims=True)

    lane = lax.broadcasted_iota(jnp.int32, (samples, block), 1)
    row = lax.broadcasted_iota(jnp.int32, (samples, block), 0)

    def fill(part, columns):
        spread = jnp.zeros((samples, block), jnp.float32)
        for v, column in enumerate(columns):
            spread = jnp.where(lane // rows == v, column, spread)
        spread = jnp.where(lane % rows == row % rows, spread, 0.0)
        for b in range(ranks):
            part[b] = jnp.sum(spread[b * rows : (b + 1) * rows], axis=0, keepdims=True)

    def send_part(part, target):
        def one(k, carry):
            rank = lax.rem(blk + k, ranks)
            slot = lax.rem(target * ranks + rank - me + total, total) - 1
            pltpu.make_async_remote_copy(
                src_ref=part.at[rank],
                dst_ref=inbox.at[slot],
                send_sem=part_sem.at[0],
                recv_sem=part_sem.at[1],
                device_id=(target, rank),
                device_id_type=MESH,
            ).start()
            return carry

        lax.fori_loop(jnp.where(sect == target, 1, 0), ranks, one, 0)

    fill(part0, [norm_stay, norm_raised])
    send_part(part0, 0)

    scales = [lax.rsqrt(norm_stay / part_width + EPS), lax.rsqrt(norm_raised / part_width + EPS)]

    def halves(value):
        high = value.astype(jnp.bfloat16)
        low = (value - high.astype(jnp.float32)).astype(jnp.bfloat16)
        return jnp.concatenate([high, low], axis=1)

    @pl.when(sect == 1)
    def _():
        own_t1.wait()

    sums = [[jnp.zeros((samples, block), jnp.float32) for _ in range(2)] for _ in range(2)]
    for j in range(half + 1):
        if j == half:
            tens_to_zero(j).wait_recv()
        else:

            @pl.when(sect == 0)
            def _():
                tens_to_zero(j).wait_recv()

        both = jnp.concatenate([t1[0, j], t1[1, j]], axis=1)
        twice = jnp.concatenate([both, both], axis=0)
        for first in range(2):
            source = j - first
            if source < 0 or source == half:
                continue
            value = images[source, :, first * block : (first + 1) * block] * scales[first]
            image = jnp.dot(halves(value), twice, preferred_element_type=jnp.float32)
            for second in range(2):
                piece = image[:, second * block : (second + 1) * block]
                sums[first][second] += piece * piece
    columns = [norm_stay, norm_raised]
    for second in range(2):
        for first in range(2):
            columns.append(jnp.sum(sums[first][second], axis=1, keepdims=True))
    fill(part1, columns)
    own_bits = pltpu.roll(bits_v[...], 6 * rows, 1)[0:1]
    part1[blk] = part1[blk] + jnp.where(sect == 0, own_bits, 0.0)
    send_part(part1, 1)

    pltpu.make_async_copy(inbox, inbox, part_sem.at[1]).wait()
    stack[0:1, :] = jnp.where(sect == 0, part0[blk], part1[blk])
    for k in range(total - 1):
        stack[k + 1 : k + 2, :] = inbox[k]
    all_parts = stack[...]
    sums_all = jnp.sum(all_parts, axis=0, keepdims=True)
    here = bits_v[...] == 1.0

    def value(source, v):
        wide = jnp.broadcast_to(source, (8, block))
        return wide if v == 0 else pltpu.roll(wide, block - v * rows, 1)

    norm_zero, norm_one = value(sums_all, 0), value(sums_all, 1)

    @pl.when(sect == 0)
    def _():
        prob = jnp.where(here, norm_one, norm_zero) / (norm_zero + norm_one)
        out_ref[0:1, :] = prob[0:1]
        out_ref[1:2, :] = jnp.log(prob)[0:1]

    @pl.when(sect == 1)
    def _():
        weight = (all_parts / part_width + EPS) / (sums_all / width + EPS)
        where = lax.broadcasted_iota(jnp.int32, (total, block), 1)
        weight = jnp.where(
            where < 4 * rows, pltpu.roll(weight, 2 * rows, 1), pltpu.roll(weight, 4 * rows, 1)
        )
        later = jnp.sum(all_parts * weight, axis=0, keepdims=True)
        before = value(sums_all, 6) == 1.0
        prob0 = jnp.where(before, norm_one, norm_zero) / (norm_zero + norm_one)
        zero = jnp.where(before, value(later, 3), value(later, 2))
        one = jnp.where(before, value(later, 5), value(later, 4))
        prob = jnp.where(here, one, zero) / (zero + one)
        out_ref[0:1, :] = prob[0:1]
        out_ref[1:2, :] = (jnp.log(prob0) + jnp.log(prob))[0:1]

    pltpu.make_async_copy(others, others, left_sem.at[0]).wait()
    pltpu.make_async_copy(inbox, inbox, part_sem.at[0]).wait()

    @pl.when(sect == 0)
    def _():
        for h in range(half):
            tens_to_one(h).wait_send()

    @pl.when(sect == 1)
    def _():
        for j in range(half + 1):
            tens_to_zero(j).wait_send()
        tens_back.wait_send()


def body_pair(ranks, bits, labels, left, tensors):
    rows = bits.shape[1]
    count_blocks = labels.shape[0]
    block = tensors.shape[-1]
    group = tensors.shape[2]
    half = group // 2
    vmem = pl.BlockSpec(memory_space=pltpu.VMEM)
    hbm = pl.BlockSpec(memory_space=pl.ANY)
    dma = pltpu.SemaphoreType.DMA
    scored = pl.pallas_call(
        functools.partial(pair_kernel, ranks),
        out_shape=pltpu.VMEM((2, block), jnp.float32),
        in_specs=[hbm, hbm, hbm, hbm],
        out_specs=vmem,
        scratch_shapes=[
            pltpu.VMEM(bits.shape, jnp.int32),
            pltpu.VMEM(labels.shape, jnp.int32),
            pltpu.VMEM(left.shape, jnp.bfloat16),
            pltpu.VMEM((count_blocks, rows, block), jnp.bfloat16),
            pltpu.VMEM((1, count_blocks), jnp.int32),
            pltpu.SMEM((1, count_blocks), jnp.int32),
            pltpu.VMEM((ranks, rows, half * block), jnp.bfloat16),
            pltpu.VMEM((ranks * rows, half * block), jnp.bfloat16),
            pltpu.VMEM((half, ranks * rows, 2 * block), jnp.float32),
            pltpu.VMEM((2, half, block, block), jnp.bfloat16),
            pltpu.VMEM((2, half + 1, block, block), jnp.bfloat16),
            pltpu.VMEM((ranks, 1, block), jnp.float32),
            pltpu.VMEM((ranks, 1, block), jnp.float32),
            pltpu.VMEM((2 * ranks - 1, 1, block), jnp.float32),
            pltpu.VMEM((2 * ranks, block), jnp.float32),
            pltpu.VMEM((8, block), jnp.float32),
            dma((5,)),
            dma((half,)),
            dma((half,)),
            dma((half + 2,)),
            dma((half + 1,)),
            dma((2,)),
            dma((2,)),
        ],
        compiler_params=pltpu.CompilerParams(
            collective_id=0, has_side_effects=True, vmem_limit_bytes=60 * 1024 * 1024
        ),
        name="score_pair",
    )(bits, labels, left, tensors)
    return scored[0:1, :rows], scored[1:2, :rows]


def solution(mesh):
    in_specs = (P("sect", "blk"), P(), P("blk", None), P("sect", None, "blk", None, None))
    out_specs = (P("sect", "blk"), P("sect", "blk"))
    if mesh.shape["sect"] == 2:
        body = functools.partial(body_pair, mesh.shape["blk"])
    else:
        body = body_many
    return jax.shard_map(body, mesh=mesh, in_specs=in_specs, out_specs=out_specs, check_vma=False)
```

```python
import functools

import jax
import jax.numpy as jnp
from jax import lax
from jax.experimental import pallas as pl
from jax.experimental.pallas import tpu as pltpu
from jax.sharding import PartitionSpec as P

MESH = pl.DeviceIdType.MESH
EPS = 1e-06


def passed_along(value, axis, steps):
    count = lax.axis_size(axis)
    first, last = (max(0, -steps), min(count, count - steps))
    return lax.ppermute(value, axis, [(source, source + steps) for source in range(first, last)])


def charge_order(labels, left, block):
    count_blocks = labels.shape[0]
    samples_here = left.shape[0]
    blocks = left.reshape(samples_here, count_blocks, block)
    index = jnp.arange(count_blocks, dtype=jnp.int32)
    pick = (labels[None, :] == index[:, None]).astype(jnp.bfloat16)
    ordered = jnp.einsum("ci,rik->rck", pick, blocks, preferred_element_type=jnp.float32)
    return ordered.astype(jnp.bfloat16)


def site_images(state, weights, block):
    count_rows = state.shape[0]
    blocks = state.reshape(count_rows, weights.shape[1], block)
    return jnp.einsum(
        "rck,bckl->brcl",
        blocks,
        weights,
        preferred_element_type=jnp.float32,
        precision=lax.Precision.HIGHEST,
    )


def run_sections(start_rows, site_bits, advance, count):
    segment = lax.axis_index("sect")
    segments = lax.axis_size("sect")
    mrows = start_rows.shape[1]

    def one_step(step, carry):
        state, total, prob_out, log_out = carry
        group = step - segment
        valid = (group >= 0) & (group < count)
        slot = jnp.clip(group, 0, count - 1)
        first = segment == 0
        start_now = lax.dynamic_index_in_dim(start_rows, slot, 0, keepdims=False)
        state = jnp.where(first, start_now, state)
        total = jnp.where(first, jnp.zeros_like(total), total)
        bit_rows = lax.dynamic_index_in_dim(site_bits, slot, 0, keepdims=False)
        prob, next_state = advance(state, bit_rows)
        total = total + jnp.log(prob)
        old_prob = lax.dynamic_index_in_dim(prob_out, slot, 0, keepdims=False)
        old_log = lax.dynamic_index_in_dim(log_out, slot, 0, keepdims=False)
        prob_out = lax.dynamic_update_index_in_dim(
            prob_out, jnp.where(valid, prob, old_prob), slot, 0
        )
        log_out = lax.dynamic_update_index_in_dim(
            log_out, jnp.where(valid, total, old_log), slot, 0
        )
        state, total = passed_along((next_state, total), "sect", 1)
        return (state, total, prob_out, log_out)

    empty = jnp.zeros((count, mrows), jnp.float32)
    init = (start_rows[0], jnp.zeros((mrows,), jnp.float32), empty, empty)
    result = lax.fori_loop(0, count + segments - 1, one_step, init)
    return (result[2], result[3])


def body_many(bits, labels, left, tensors):
    block = tensors.shape[-1]
    count_blocks = labels.shape[0]
    width = count_blocks * block
    rows = bits.shape[1]
    ordered = charge_order(labels, left, block)
    whole = lax.all_gather(tensors, "blk", axis=2, tiled=True)[0]

    def advance(state, bit_rows):
        image = site_images(state, whole, block)
        stay = image[0]
        raised = jnp.roll(image[1], 1, axis=1)
        norm_zero = jnp.sum(stay * stay, axis=(1, 2))
        norm_one = jnp.sum(raised * raised, axis=(1, 2))
        choose = bit_rows == 1
        chosen_norm = jnp.where(choose, norm_one, norm_zero)
        prob = chosen_norm / (norm_zero + norm_one)
        chosen = jnp.where(choose[:, None, None], raised, stay)
        scaled = chosen * lax.rsqrt(chosen_norm / width + EPS)[:, None, None]
        return (prob, scaled.reshape(state.shape[0], width))

    start_rows = ordered.astype(jnp.float32).reshape(1, rows, width)
    return run_sections(start_rows, bits[0].reshape(1, rows), advance, 1)


def pair_kernel(
    ranks,
    bits_ref,
    labels_ref,
    left_ref,
    tens_ref,
    out_ref,
    bits_i,
    labels_v,
    left_v,
    left_b,
    inv_v,
    inv_s,
    ordered,
    state,
    images,
    t0,
    t1,
    part0,
    part1,
    inbox,
    stack,
    bits_v,
    local_sem,
    t0_send,
    t0_recv,
    t1_send,
    t1_recv,
    left_sem,
    part_sem,
):
    sect = lax.axis_index("sect")
    blk = lax.axis_index("blk")
    me = sect * ranks + blk
    total = 2 * ranks
    rows = bits_ref.shape[1]
    block = tens_ref.shape[-1]
    group = tens_ref.shape[2]
    half = group // 2
    count_blocks = group * ranks
    samples = rows * ranks
    width = count_blocks * block
    part_width = half * block

    labels_copy = pltpu.make_async_copy(labels_ref, labels_v, local_sem.at[3])
    labels_copy.start()
    left_copy = pltpu.make_async_copy(left_ref, left_v, local_sem.at[0])
    left_copy.start()
    bits_copy = pltpu.make_async_copy(bits_ref, bits_i, local_sem.at[4])
    bits_copy.start()
    own_t0 = pltpu.make_async_copy(tens_ref.at[0, :, pl.ds(0, half)], t0, local_sem.at[1])
    own_t1 = pltpu.make_async_copy(
        tens_ref.at[0, :, pl.ds(half, half)], t1.at[:, pl.ds(0, half)], local_sem.at[1]
    )

    @pl.when(sect == 0)
    def _():
        own_t0.start()

    @pl.when(sect == 1)
    def _():
        own_t1.start()

    barrier = pltpu.get_barrier_semaphore()

    far_first = sorted(range(1, ranks), key=lambda k: abs(k - ranks // 2))

    pl.semaphore_signal(barrier, inc=1, device_id=(1 - sect, blk), device_id_type=MESH)
    for k in far_first:
        pl.semaphore_signal(
            barrier, inc=1, device_id=(sect, lax.rem(blk + k, ranks)), device_id_type=MESH
        )

    labels_copy.wait()
    labels = jnp.broadcast_to(labels_v[...].reshape(1, count_blocks), (count_blocks, count_blocks))
    place = lax.broadcasted_iota(jnp.int32, (count_blocks, count_blocks), 0)
    charge = lax.broadcasted_iota(jnp.int32, (count_blocks, count_blocks), 1)
    inv_v[...] = jnp.max(jnp.where(labels.T == charge, place, 0), axis=0, keepdims=True)
    inv_copy = pltpu.make_async_copy(inv_v, inv_s, local_sem.at[2])
    inv_copy.start()
    left_copy.wait()
    for i in range(count_blocks):
        left_b[i] = left_v[:, i * block : (i + 1) * block]
    bits_v[...] = jnp.zeros_like(bits_v)
    bits_copy.wait()
    bits_v[0:1, 0:rows] = bits_i[...].astype(jnp.float32)
    inv_copy.wait()
    for b in range(ranks):
        for h in range(half):
            where = inv_s[0, group * b + half * sect + h]
            ordered[b, :, h * block : (h + 1) * block] = left_b[where]

    pl.semaphore_wait(barrier, ranks)

    def tens_to_one(h):
        return pltpu.make_async_remote_copy(
            src_ref=tens_ref.at[0, :, pl.ds(half + h, 1)],
            dst_ref=t0.at[:, pl.ds(h, 1)],
            send_sem=t0_send.at[h],
            recv_sem=t0_recv.at[h],
            device_id=(1, blk),
            device_id_type=MESH,
        )

    def tens_to_zero(j):
        return pltpu.make_async_remote_copy(
            src_ref=tens_ref.at[0, :, pl.ds(j, 1)],
            dst_ref=t1.at[:, pl.ds(j, 1)],
            send_sem=t1_send.at[j],
            recv_sem=t1_recv.at[j],
            device_id=(0, blk),
            device_id_type=MESH,
        )

    tens_back = pltpu.make_async_remote_copy(
        src_ref=tens_ref.at[0, :, pl.ds(0, 1)],
        dst_ref=t1.at[:, pl.ds(half, 1)],
        send_sem=t1_send.at[half + 1],
        recv_sem=t1_recv.at[half],
        device_id=(1, lax.rem(blk + ranks - 1, ranks)),
        device_id_type=MESH,
    )

    mine = pl.ds(pl.multiple_of(blk * rows, rows), rows)

    def send_left(k):
        other = lax.rem(blk + k, ranks)
        pltpu.make_async_remote_copy(
            src_ref=ordered.at[other],
            dst_ref=state.at[mine],
            send_sem=left_sem.at[0],
            recv_sem=left_sem.at[1],
            device_id=(sect, other),
            device_id_type=MESH,
        ).start()

    for i, k in enumerate(far_first):
        send_left(k)
        if i % 2 == 1 and i // 2 < half:

            @pl.when(sect == 0)
            def _():
                tens_to_one(i // 2).start()

            @pl.when(sect == 1)
            def _():
                tens_to_zero(i // 2).start()

    @pl.when(sect == 1)
    def _():
        tens_to_zero(half).start()
        tens_back.start()

    state[mine, :] = ordered[blk]

    others = state.at[pl.ds(0, (ranks - 1) * rows)]
    pltpu.make_async_copy(others, others, left_sem.at[1]).wait()

    @pl.when(sect == 0)
    def _():
        own_t0.wait()

    sum_stay = jnp.zeros((samples, block), jnp.float32)
    sum_raised = jnp.zeros((samples, block), jnp.float32)
    for h in range(half):

        @pl.when(sect == 1)
        def _():
            tens_to_one(h).wait_recv()

        both = jnp.concatenate([t0[0, h], t0[1, h]], axis=1)
        image = jnp.dot(
            state[:, h * block : (h + 1) * block], both, preferred_element_type=jnp.float32
        )
        images[h] = image
        stay, raised = image[:, :block], image[:, block:]
        sum_stay += stay * stay
        sum_raised += raised * raised
    norm_stay = jnp.sum(sum_stay, axis=1, keepdims=True)
    norm_raised = jnp.sum(sum_raised, axis=1, keepdims=True)

    lane = lax.broadcasted_iota(jnp.int32, (samples, block), 1)
    row = lax.broadcasted_iota(jnp.int32, (samples, block), 0)

    def fill(part, columns):
        spread = jnp.zeros((samples, block), jnp.float32)
        for v, column in enumerate(columns):
            spread = jnp.where(lane // rows == v, column, spread)
        spread = jnp.where(lane % rows == row % rows, spread, 0.0)
        for b in range(ranks):
            part[b] = jnp.sum(spread[b * rows : (b + 1) * rows], axis=0, keepdims=True)

    def send_part(part, target):
        def one(k):
            rank = lax.rem(blk + k, ranks)
            slot = lax.rem(target * ranks + rank - me + total, total) - 1
            pltpu.make_async_remote_copy(
                src_ref=part.at[rank],
                dst_ref=inbox.at[slot],
                send_sem=part_sem.at[0],
                recv_sem=part_sem.at[1],
                device_id=(target, rank),
                device_id_type=MESH,
            ).start()

        for k in far_first:
            one(k)

        @pl.when(sect != target)
        def _():
            one(0)

    fill(part0, [norm_stay, norm_raised])
    send_part(part0, 0)

    scales = [lax.rsqrt(norm_stay / part_width + EPS), lax.rsqrt(norm_raised / part_width + EPS)]

    def halves(value):
        high = value.astype(jnp.bfloat16)
        low = (value - high.astype(jnp.float32)).astype(jnp.bfloat16)
        return jnp.concatenate([high, low], axis=1)

    @pl.when(sect == 1)
    def _():
        own_t1.wait()

    sums = [[jnp.zeros((samples, block), jnp.float32) for _ in range(2)] for _ in range(2)]
    for j in range(half + 1):
        if j == half:
            tens_to_zero(j).wait_recv()
        else:

            @pl.when(sect == 0)
            def _():
                tens_to_zero(j).wait_recv()

        both = jnp.concatenate([t1[0, j], t1[1, j]], axis=1)
        twice = jnp.concatenate([both, both], axis=0)
        firsts = [first for first in range(2) if 0 <= j - first < half]
        values = [
            images[j - first, :, first * block : (first + 1) * block] * scales[first]
            for first in firsts
        ]
        image = jnp.dot(
            jnp.concatenate([halves(value) for value in values], axis=0),
            twice,
            preferred_element_type=jnp.float32,
        )
        for i, first in enumerate(firsts):
            for second in range(2):
                piece = image[
                    i * samples : (i + 1) * samples, second * block : (second + 1) * block
                ]
                sums[first][second] += piece * piece
    columns = [norm_stay, norm_raised]
    for second in range(2):
        for first in range(2):
            columns.append(jnp.sum(sums[first][second], axis=1, keepdims=True))
    fill(part1, columns)
    own_bits = pltpu.roll(bits_v[...], 6 * rows, 1)[0:1]
    part1[blk] = part1[blk] + jnp.where(sect == 0, own_bits, 0.0)
    send_part(part1, 1)

    pltpu.make_async_copy(inbox, inbox, part_sem.at[1]).wait()
    stack[0:1, :] = jnp.where(sect == 0, part0[blk], part1[blk])
    for k in range(total - 1):
        stack[k + 1 : k + 2, :] = inbox[k]
    all_parts = stack[...]
    sums_all = jnp.sum(all_parts, axis=0, keepdims=True)
    here = bits_v[...] == 1.0

    def value(source, v):
        wide = jnp.broadcast_to(source, (8, block))
        return wide if v == 0 else pltpu.roll(wide, block - v * rows, 1)

    norm_zero, norm_one = value(sums_all, 0), value(sums_all, 1)

    @pl.when(sect == 0)
    def _():
        prob = jnp.where(here, norm_one, norm_zero) / (norm_zero + norm_one)
        out_ref[0:1, :] = prob[0:1]
        out_ref[1:2, :] = jnp.log(prob)[0:1]

    @pl.when(sect == 1)
    def _():
        weight = (all_parts / part_width + EPS) / (sums_all / width + EPS)
        where = lax.broadcasted_iota(jnp.int32, (total, block), 1)
        weight = jnp.where(
            where < 4 * rows, pltpu.roll(weight, 2 * rows, 1), pltpu.roll(weight, 4 * rows, 1)
        )
        later = jnp.sum(all_parts * weight, axis=0, keepdims=True)
        before = value(sums_all, 6) == 1.0
        prob0 = jnp.where(before, norm_one, norm_zero) / (norm_zero + norm_one)
        zero = jnp.where(before, value(later, 3), value(later, 2))
        one = jnp.where(before, value(later, 5), value(later, 4))
        prob = jnp.where(here, one, zero) / (zero + one)
        out_ref[0:1, :] = prob[0:1]
        out_ref[1:2, :] = (jnp.log(prob0) + jnp.log(prob))[0:1]

    pltpu.make_async_copy(others, others, left_sem.at[0]).wait()
    pltpu.make_async_copy(inbox, inbox, part_sem.at[0]).wait()

    @pl.when(sect == 0)
    def _():
        for h in range(half):
            tens_to_one(h).wait_send()

    @pl.when(sect == 1)
    def _():
        for j in range(half + 1):
            tens_to_zero(j).wait_send()
        tens_back.wait_send()


def body_pair(ranks, bits, labels, left, tensors):
    rows = bits.shape[1]
    count_blocks = labels.shape[0]
    block = tensors.shape[-1]
    group = tensors.shape[2]
    half = group // 2
    vmem = pl.BlockSpec(memory_space=pltpu.VMEM)
    hbm = pl.BlockSpec(memory_space=pl.ANY)
    dma = pltpu.SemaphoreType.DMA
    scored = pl.pallas_call(
        functools.partial(pair_kernel, ranks),
        out_shape=pltpu.VMEM((2, block), jnp.float32),
        in_specs=[hbm, hbm, hbm, hbm],
        out_specs=vmem,
        scratch_shapes=[
            pltpu.VMEM(bits.shape, jnp.int32),
            pltpu.VMEM(labels.shape, jnp.int32),
            pltpu.VMEM(left.shape, jnp.bfloat16),
            pltpu.VMEM((count_blocks, rows, block), jnp.bfloat16),
            pltpu.VMEM((1, count_blocks), jnp.int32),
            pltpu.SMEM((1, count_blocks), jnp.int32),
            pltpu.VMEM((ranks, rows, half * block), jnp.bfloat16),
            pltpu.VMEM((ranks * rows, half * block), jnp.bfloat16),
            pltpu.VMEM((half, ranks * rows, 2 * block), jnp.float32),
            pltpu.VMEM((2, half, block, block), jnp.bfloat16),
            pltpu.VMEM((2, half + 1, block, block), jnp.bfloat16),
            pltpu.VMEM((ranks, 1, block), jnp.float32),
            pltpu.VMEM((ranks, 1, block), jnp.float32),
            pltpu.VMEM((2 * ranks - 1, 1, block), jnp.float32),
            pltpu.VMEM((2 * ranks, block), jnp.float32),
            pltpu.VMEM((8, block), jnp.float32),
            dma((5,)),
            dma((half,)),
            dma((half,)),
            dma((half + 2,)),
            dma((half + 1,)),
            dma((2,)),
            dma((2,)),
        ],
        compiler_params=pltpu.CompilerParams(
            collective_id=0, has_side_effects=True, vmem_limit_bytes=60 * 1024 * 1024
        ),
        name="score_pair",
    )(bits, labels, left, tensors)
    return scored[0:1, :rows], scored[1:2, :rows]


def solution(mesh):
    in_specs = (P("sect", "blk"), P(), P("blk", None), P("sect", None, "blk", None, None))
    out_specs = (P("sect", "blk"), P("sect", "blk"))
    if mesh.shape["sect"] == 2:
        body = functools.partial(body_pair, mesh.shape["blk"])
    else:
        body = body_many
    return jax.shard_map(body, mesh=mesh, in_specs=in_specs, out_specs=out_specs, check_vma=False)
```

```python
import functools

import jax
import jax.numpy as jnp
from jax import lax
from jax.experimental import pallas as pl
from jax.experimental.pallas import tpu as pltpu
from jax.sharding import PartitionSpec as P

MESH = pl.DeviceIdType.MESH
EPS = 1e-06


def passed_along(value, axis, steps):
    count = lax.axis_size(axis)
    first, last = (max(0, -steps), min(count, count - steps))
    return lax.ppermute(value, axis, [(source, source + steps) for source in range(first, last)])


def charge_order(labels, left, block):
    count_blocks = labels.shape[0]
    samples_here = left.shape[0]
    blocks = left.reshape(samples_here, count_blocks, block)
    index = jnp.arange(count_blocks, dtype=jnp.int32)
    pick = (labels[None, :] == index[:, None]).astype(jnp.bfloat16)
    ordered = jnp.einsum("ci,rik->rck", pick, blocks, preferred_element_type=jnp.float32)
    return ordered.astype(jnp.bfloat16)


def site_images(state, weights, block):
    count_rows = state.shape[0]
    blocks = state.reshape(count_rows, weights.shape[1], block)
    return jnp.einsum(
        "rck,bckl->brcl",
        blocks,
        weights,
        preferred_element_type=jnp.float32,
        precision=lax.Precision.HIGHEST,
    )


def run_sections(start_rows, site_bits, advance, count):
    segment = lax.axis_index("sect")
    segments = lax.axis_size("sect")
    mrows = start_rows.shape[1]

    def one_step(step, carry):
        state, total, prob_out, log_out = carry
        group = step - segment
        valid = (group >= 0) & (group < count)
        slot = jnp.clip(group, 0, count - 1)
        first = segment == 0
        start_now = lax.dynamic_index_in_dim(start_rows, slot, 0, keepdims=False)
        state = jnp.where(first, start_now, state)
        total = jnp.where(first, jnp.zeros_like(total), total)
        bit_rows = lax.dynamic_index_in_dim(site_bits, slot, 0, keepdims=False)
        prob, next_state = advance(state, bit_rows)
        total = total + jnp.log(prob)
        old_prob = lax.dynamic_index_in_dim(prob_out, slot, 0, keepdims=False)
        old_log = lax.dynamic_index_in_dim(log_out, slot, 0, keepdims=False)
        prob_out = lax.dynamic_update_index_in_dim(
            prob_out, jnp.where(valid, prob, old_prob), slot, 0
        )
        log_out = lax.dynamic_update_index_in_dim(
            log_out, jnp.where(valid, total, old_log), slot, 0
        )
        state, total = passed_along((next_state, total), "sect", 1)
        return (state, total, prob_out, log_out)

    empty = jnp.zeros((count, mrows), jnp.float32)
    init = (start_rows[0], jnp.zeros((mrows,), jnp.float32), empty, empty)
    result = lax.fori_loop(0, count + segments - 1, one_step, init)
    return (result[2], result[3])


def body_many(bits, labels, left, tensors):
    block = tensors.shape[-1]
    count_blocks = labels.shape[0]
    width = count_blocks * block
    rows = bits.shape[1]
    ordered = charge_order(labels, left, block)
    whole = lax.all_gather(tensors, "blk", axis=2, tiled=True)[0]

    def advance(state, bit_rows):
        image = site_images(state, whole, block)
        stay = image[0]
        raised = jnp.roll(image[1], 1, axis=1)
        norm_zero = jnp.sum(stay * stay, axis=(1, 2))
        norm_one = jnp.sum(raised * raised, axis=(1, 2))
        choose = bit_rows == 1
        chosen_norm = jnp.where(choose, norm_one, norm_zero)
        prob = chosen_norm / (norm_zero + norm_one)
        chosen = jnp.where(choose[:, None, None], raised, stay)
        scaled = chosen * lax.rsqrt(chosen_norm / width + EPS)[:, None, None]
        return (prob, scaled.reshape(state.shape[0], width))

    start_rows = ordered.astype(jnp.float32).reshape(1, rows, width)
    return run_sections(start_rows, bits[0].reshape(1, rows), advance, 1)


def pair_kernel(
    ranks,
    bits_ref,
    labels_ref,
    left_ref,
    tens_ref,
    out_ref,
    bits_i,
    labels_v,
    left_v,
    left_b,
    inv_v,
    inv_s,
    ordered,
    state,
    images,
    t0,
    t1,
    part0,
    part1,
    inbox,
    stack,
    bits_v,
    local_sem,
    t0_send,
    t0_recv,
    t1_send,
    t1_recv,
    left_sem,
    part_sem,
):
    sect = lax.axis_index("sect")
    blk = lax.axis_index("blk")
    me = sect * ranks + blk
    total = 2 * ranks
    rows = bits_ref.shape[1]
    block = tens_ref.shape[-1]
    group = tens_ref.shape[2]
    half = group // 2
    count_blocks = group * ranks
    samples = rows * ranks
    width = count_blocks * block
    part_width = half * block

    labels_copy = pltpu.make_async_copy(labels_ref, labels_v, local_sem.at[3])
    labels_copy.start()
    left_copy = pltpu.make_async_copy(left_ref, left_v, local_sem.at[0])
    left_copy.start()
    bits_copy = pltpu.make_async_copy(bits_ref, bits_i, local_sem.at[4])
    bits_copy.start()
    own_t0 = pltpu.make_async_copy(tens_ref.at[0, :, pl.ds(0, half)], t0, local_sem.at[1])
    own_t1 = pltpu.make_async_copy(
        tens_ref.at[0, :, pl.ds(half, half)], t1.at[:, pl.ds(0, half)], local_sem.at[1]
    )

    @pl.when(sect == 0)
    def _():
        own_t0.start()

    @pl.when(sect == 1)
    def _():
        own_t1.start()

    barrier = pltpu.get_barrier_semaphore()

    far_first = sorted(range(1, ranks), key=lambda k: abs(k - ranks // 2))

    pl.semaphore_signal(barrier, inc=1, device_id=(1 - sect, blk), device_id_type=MESH)
    for k in far_first:
        pl.semaphore_signal(
            barrier, inc=1, device_id=(sect, lax.rem(blk + k, ranks)), device_id_type=MESH
        )

    labels_copy.wait()
    labels = jnp.broadcast_to(labels_v[...].reshape(1, count_blocks), (count_blocks, count_blocks))
    place = lax.broadcasted_iota(jnp.int32, (count_blocks, count_blocks), 0)
    charge = lax.broadcasted_iota(jnp.int32, (count_blocks, count_blocks), 1)
    inv_v[...] = jnp.max(jnp.where(labels.T == charge, place, 0), axis=0, keepdims=True)
    inv_copy = pltpu.make_async_copy(inv_v, inv_s, local_sem.at[2])
    inv_copy.start()
    left_copy.wait()
    for i in range(count_blocks):
        left_b[i] = left_v[:, i * block : (i + 1) * block]
    bits_v[...] = jnp.zeros_like(bits_v)
    bits_copy.wait()
    bits_v[0:1, 0:rows] = bits_i[...].astype(jnp.float32)
    pl.semaphore_wait(barrier, ranks)

    pieces0 = [(h, min(2, half - h)) for h in range(0, half, 2)]
    pieces1 = [(j, min(2, half + 1 - j)) for j in range(0, half + 1, 2)]

    def tens_to_one(i):
        first, many = pieces0[i]
        return pltpu.make_async_remote_copy(
            src_ref=tens_ref.at[0, :, pl.ds(half + first, many)],
            dst_ref=t0.at[:, pl.ds(first, many)],
            send_sem=t0_send.at[i],
            recv_sem=t0_recv.at[i],
            device_id=(1, blk),
            device_id_type=MESH,
        )

    def tens_to_zero(i):
        first, many = pieces1[i]
        return pltpu.make_async_remote_copy(
            src_ref=tens_ref.at[0, :, pl.ds(first, many)],
            dst_ref=t1.at[:, pl.ds(first, many)],
            send_sem=t1_send.at[i],
            recv_sem=t1_recv.at[i],
            device_id=(0, blk),
            device_id_type=MESH,
        )

    def send_piece(i):
        if i < len(pieces0):

            @pl.when(sect == 0)
            def _():
                tens_to_one(i).start()

        @pl.when(sect == 1)
        def _():
            tens_to_zero(i).start()

    tens_back = pltpu.make_async_remote_copy(
        src_ref=tens_ref.at[0, :, pl.ds(0, 1)],
        dst_ref=t1.at[:, pl.ds(half, 1)],
        send_sem=t1_send.at[half + 1],
        recv_sem=t1_recv.at[half + 1],
        device_id=(1, lax.rem(blk + ranks - 1, ranks)),
        device_id_type=MESH,
    )

    send_piece(0)
    inv_copy.wait()
    for b in range(ranks):
        for h in range(half):
            where = inv_s[0, group * b + half * sect + h]
            ordered[b, :, h * block : (h + 1) * block] = left_b[where]

    mine = pl.ds(pl.multiple_of(blk * rows, rows), rows)

    def send_left(k):
        other = lax.rem(blk + k, ranks)
        pltpu.make_async_remote_copy(
            src_ref=ordered.at[other],
            dst_ref=state.at[mine],
            send_sem=left_sem.at[0],
            recv_sem=left_sem.at[1],
            device_id=(sect, other),
            device_id_type=MESH,
        ).start()

    for i, k in enumerate(far_first):
        send_left(k)
        if i % 3 == 2 and 0 < i // 3 + 1 < len(pieces1):
            send_piece(i // 3 + 1)

    @pl.when(sect == 1)
    def _():
        tens_back.start()

    state[mine, :] = ordered[blk]

    others = state.at[pl.ds(0, (ranks - 1) * rows)]
    pltpu.make_async_copy(others, others, left_sem.at[1]).wait()

    @pl.when(sect == 0)
    def _():
        own_t0.wait()

    sum_stay = jnp.zeros((samples, block), jnp.float32)
    sum_raised = jnp.zeros((samples, block), jnp.float32)
    for h in range(half):

        if any(first == h for first, _ in pieces0):

            @pl.when(sect == 1)
            def _():
                tens_to_one(h // 2).wait_recv()

        both = jnp.concatenate([t0[0, h], t0[1, h]], axis=1)
        image = jnp.dot(
            state[:, h * block : (h + 1) * block], both, preferred_element_type=jnp.float32
        )
        images[h] = image
        stay, raised = image[:, :block], image[:, block:]
        sum_stay += stay * stay
        sum_raised += raised * raised
    norm_stay = jnp.sum(sum_stay, axis=1, keepdims=True)
    norm_raised = jnp.sum(sum_raised, axis=1, keepdims=True)

    lane = lax.broadcasted_iota(jnp.int32, (samples, block), 1)
    row = lax.broadcasted_iota(jnp.int32, (samples, block), 0)

    def fill(part, columns):
        spread = jnp.zeros((samples, block), jnp.float32)
        for v, column in enumerate(columns):
            spread = jnp.where(lane // rows == v, column, spread)
        spread = jnp.where(lane % rows == row % rows, spread, 0.0)
        for b in range(ranks):
            part[b] = jnp.sum(spread[b * rows : (b + 1) * rows], axis=0, keepdims=True)

    def send_part(part, target):
        def one(k):
            rank = lax.rem(blk + k, ranks)
            slot = lax.rem(target * ranks + rank - me + total, total) - 1
            pltpu.make_async_remote_copy(
                src_ref=part.at[rank],
                dst_ref=inbox.at[slot],
                send_sem=part_sem.at[0],
                recv_sem=part_sem.at[1],
                device_id=(target, rank),
                device_id_type=MESH,
            ).start()

        for k in far_first:
            one(k)

        @pl.when(sect != target)
        def _():
            one(0)

    fill(part0, [norm_stay, norm_raised])
    send_part(part0, 0)

    scales = [lax.rsqrt(norm_stay / part_width + EPS), lax.rsqrt(norm_raised / part_width + EPS)]

    def halves(value):
        high = value.astype(jnp.bfloat16)
        low = (value - high.astype(jnp.float32)).astype(jnp.bfloat16)
        return jnp.concatenate([high, low], axis=1)

    @pl.when(sect == 1)
    def _():
        own_t1.wait()

    sums = [[jnp.zeros((samples, block), jnp.float32) for _ in range(2)] for _ in range(2)]
    for j in range(half + 1):
        if any(first == j for first, _ in pieces1):

            @pl.when(sect == 0)
            def _():
                tens_to_zero(j // 2).wait_recv()

        if j == half:

            @pl.when(sect == 1)
            def _():
                tens_back.wait_recv()

        both = jnp.concatenate([t1[0, j], t1[1, j]], axis=1)
        twice = jnp.concatenate([both, both], axis=0)
        firsts = [first for first in range(2) if 0 <= j - first < half]
        values = [
            images[j - first, :, first * block : (first + 1) * block] * scales[first]
            for first in firsts
        ]
        image = jnp.dot(
            jnp.concatenate([halves(value) for value in values], axis=0),
            twice,
            preferred_element_type=jnp.float32,
        )
        for i, first in enumerate(firsts):
            for second in range(2):
                piece = image[
                    i * samples : (i + 1) * samples, second * block : (second + 1) * block
                ]
                sums[first][second] += piece * piece
    columns = [norm_stay, norm_raised]
    for second in range(2):
        for first in range(2):
            columns.append(jnp.sum(sums[first][second], axis=1, keepdims=True))
    fill(part1, columns)
    own_bits = pltpu.roll(bits_v[...], 6 * rows, 1)[0:1]
    part1[blk] = part1[blk] + jnp.where(sect == 0, own_bits, 0.0)
    send_part(part1, 1)

    pltpu.make_async_copy(inbox, inbox, part_sem.at[1]).wait()
    stack[0:1, :] = jnp.where(sect == 0, part0[blk], part1[blk])
    for k in range(total - 1):
        stack[k + 1 : k + 2, :] = inbox[k]
    all_parts = stack[...]
    sums_all = jnp.sum(all_parts, axis=0, keepdims=True)
    here = bits_v[...] == 1.0

    def value(source, v):
        wide = jnp.broadcast_to(source, (8, block))
        return wide if v == 0 else pltpu.roll(wide, block - v * rows, 1)

    norm_zero, norm_one = value(sums_all, 0), value(sums_all, 1)

    @pl.when(sect == 0)
    def _():
        prob = jnp.where(here, norm_one, norm_zero) / (norm_zero + norm_one)
        out_ref[0:1, :] = prob[0:1]
        out_ref[1:2, :] = jnp.log(prob)[0:1]

    @pl.when(sect == 1)
    def _():
        weight = (all_parts / part_width + EPS) / (sums_all / width + EPS)
        where = lax.broadcasted_iota(jnp.int32, (total, block), 1)
        weight = jnp.where(
            where < 4 * rows, pltpu.roll(weight, 2 * rows, 1), pltpu.roll(weight, 4 * rows, 1)
        )
        later = jnp.sum(all_parts * weight, axis=0, keepdims=True)
        before = value(sums_all, 6) == 1.0
        prob0 = jnp.where(before, norm_one, norm_zero) / (norm_zero + norm_one)
        zero = jnp.where(before, value(later, 3), value(later, 2))
        one = jnp.where(before, value(later, 5), value(later, 4))
        prob = jnp.where(here, one, zero) / (zero + one)
        out_ref[0:1, :] = prob[0:1]
        out_ref[1:2, :] = (jnp.log(prob0) + jnp.log(prob))[0:1]

    pltpu.make_async_copy(others, others, left_sem.at[0]).wait()
    pltpu.make_async_copy(inbox, inbox, part_sem.at[0]).wait()

    @pl.when(sect == 0)
    def _():
        for i in range(len(pieces0)):
            tens_to_one(i).wait_send()

    @pl.when(sect == 1)
    def _():
        for i in range(len(pieces1)):
            tens_to_zero(i).wait_send()
        tens_back.wait_send()


def body_pair(ranks, bits, labels, left, tensors):
    rows = bits.shape[1]
    count_blocks = labels.shape[0]
    block = tensors.shape[-1]
    group = tensors.shape[2]
    half = group // 2
    vmem = pl.BlockSpec(memory_space=pltpu.VMEM)
    hbm = pl.BlockSpec(memory_space=pl.ANY)
    dma = pltpu.SemaphoreType.DMA
    scored = pl.pallas_call(
        functools.partial(pair_kernel, ranks),
        out_shape=pltpu.VMEM((2, block), jnp.float32),
        in_specs=[hbm, hbm, hbm, hbm],
        out_specs=vmem,
        scratch_shapes=[
            pltpu.VMEM(bits.shape, jnp.int32),
            pltpu.VMEM(labels.shape, jnp.int32),
            pltpu.VMEM(left.shape, jnp.bfloat16),
            pltpu.VMEM((count_blocks, rows, block), jnp.bfloat16),
            pltpu.VMEM((1, count_blocks), jnp.int32),
            pltpu.SMEM((1, count_blocks), jnp.int32),
            pltpu.VMEM((ranks, rows, half * block), jnp.bfloat16),
            pltpu.VMEM((ranks * rows, half * block), jnp.bfloat16),
            pltpu.VMEM((half, ranks * rows, 2 * block), jnp.float32),
            pltpu.VMEM((2, half, block, block), jnp.bfloat16),
            pltpu.VMEM((2, half + 1, block, block), jnp.bfloat16),
            pltpu.VMEM((ranks, 1, block), jnp.float32),
            pltpu.VMEM((ranks, 1, block), jnp.float32),
            pltpu.VMEM((2 * ranks - 1, 1, block), jnp.float32),
            pltpu.VMEM((2 * ranks, block), jnp.float32),
            pltpu.VMEM((8, block), jnp.float32),
            dma((5,)),
            dma((half,)),
            dma((half,)),
            dma((half + 2,)),
            dma((half + 2,)),
            dma((2,)),
            dma((2,)),
        ],
        compiler_params=pltpu.CompilerParams(
            collective_id=0, has_side_effects=True, vmem_limit_bytes=60 * 1024 * 1024
        ),
        name="score_pair",
    )(bits, labels, left, tensors)
    return scored[0:1, :rows], scored[1:2, :rows]


def solution(mesh):
    in_specs = (P("sect", "blk"), P(), P("blk", None), P("sect", None, "blk", None, None))
    out_specs = (P("sect", "blk"), P("sect", "blk"))
    if mesh.shape["sect"] == 2:
        body = functools.partial(body_pair, mesh.shape["blk"])
    else:
        body = body_many
    return jax.shard_map(body, mesh=mesh, in_specs=in_specs, out_specs=out_specs, check_vma=False)
```

```python
import functools

import jax
import jax.numpy as jnp
from jax import lax
from jax.experimental import pallas as pl
from jax.experimental.pallas import tpu as pltpu
from jax.sharding import PartitionSpec as P

MESH = pl.DeviceIdType.MESH
EPS = 1e-06


def passed_along(value, axis, steps):
    count = lax.axis_size(axis)
    first, last = (max(0, -steps), min(count, count - steps))
    return lax.ppermute(value, axis, [(source, source + steps) for source in range(first, last)])


def charge_order(labels, left, block):
    count_blocks = labels.shape[0]
    samples_here = left.shape[0]
    blocks = left.reshape(samples_here, count_blocks, block)
    index = jnp.arange(count_blocks, dtype=jnp.int32)
    pick = (labels[None, :] == index[:, None]).astype(jnp.bfloat16)
    ordered = jnp.einsum("ci,rik->rck", pick, blocks, preferred_element_type=jnp.float32)
    return ordered.astype(jnp.bfloat16)


def site_images(state, weights, block):
    count_rows = state.shape[0]
    blocks = state.reshape(count_rows, weights.shape[1], block)
    return jnp.einsum(
        "rck,bckl->brcl",
        blocks,
        weights,
        preferred_element_type=jnp.float32,
        precision=lax.Precision.HIGHEST,
    )


def run_sections(start_rows, site_bits, advance, count):
    segment = lax.axis_index("sect")
    segments = lax.axis_size("sect")
    mrows = start_rows.shape[1]

    def one_step(step, carry):
        state, total, prob_out, log_out = carry
        group = step - segment
        valid = (group >= 0) & (group < count)
        slot = jnp.clip(group, 0, count - 1)
        first = segment == 0
        start_now = lax.dynamic_index_in_dim(start_rows, slot, 0, keepdims=False)
        state = jnp.where(first, start_now, state)
        total = jnp.where(first, jnp.zeros_like(total), total)
        bit_rows = lax.dynamic_index_in_dim(site_bits, slot, 0, keepdims=False)
        prob, next_state = advance(state, bit_rows)
        total = total + jnp.log(prob)
        old_prob = lax.dynamic_index_in_dim(prob_out, slot, 0, keepdims=False)
        old_log = lax.dynamic_index_in_dim(log_out, slot, 0, keepdims=False)
        prob_out = lax.dynamic_update_index_in_dim(
            prob_out, jnp.where(valid, prob, old_prob), slot, 0
        )
        log_out = lax.dynamic_update_index_in_dim(
            log_out, jnp.where(valid, total, old_log), slot, 0
        )
        state, total = passed_along((next_state, total), "sect", 1)
        return (state, total, prob_out, log_out)

    empty = jnp.zeros((count, mrows), jnp.float32)
    init = (start_rows[0], jnp.zeros((mrows,), jnp.float32), empty, empty)
    result = lax.fori_loop(0, count + segments - 1, one_step, init)
    return (result[2], result[3])


def body_many(bits, labels, left, tensors):
    block = tensors.shape[-1]
    count_blocks = labels.shape[0]
    width = count_blocks * block
    rows = bits.shape[1]
    ordered = charge_order(labels, left, block)
    whole = lax.all_gather(tensors, "blk", axis=2, tiled=True)[0]

    def advance(state, bit_rows):
        image = site_images(state, whole, block)
        stay = image[0]
        raised = jnp.roll(image[1], 1, axis=1)
        norm_zero = jnp.sum(stay * stay, axis=(1, 2))
        norm_one = jnp.sum(raised * raised, axis=(1, 2))
        choose = bit_rows == 1
        chosen_norm = jnp.where(choose, norm_one, norm_zero)
        prob = chosen_norm / (norm_zero + norm_one)
        chosen = jnp.where(choose[:, None, None], raised, stay)
        scaled = chosen * lax.rsqrt(chosen_norm / width + EPS)[:, None, None]
        return (prob, scaled.reshape(state.shape[0], width))

    start_rows = ordered.astype(jnp.float32).reshape(1, rows, width)
    return run_sections(start_rows, bits[0].reshape(1, rows), advance, 1)


def pair_kernel(
    ranks,
    bits_ref,
    labels_ref,
    left_ref,
    tens_ref,
    out_ref,
    bits_i,
    labels_v,
    left_v,
    left_b,
    inv_v,
    inv_s,
    ordered,
    state,
    images,
    sums,
    t0,
    t1,
    part0,
    part1,
    inbox,
    stack,
    bits_v,
    local_sem,
    t0_send,
    t0_recv,
    t1_send,
    t1_recv,
    left_sem,
    part_sem,
):
    sect = lax.axis_index("sect")
    blk = lax.axis_index("blk")
    me = sect * ranks + blk
    total = 2 * ranks
    rows = bits_ref.shape[1]
    block = tens_ref.shape[-1]
    group = tens_ref.shape[2]
    half = group // 2
    count_blocks = group * ranks
    samples = rows * ranks
    width = count_blocks * block
    part_width = half * block

    labels_copy = pltpu.make_async_copy(labels_ref, labels_v, local_sem.at[3])
    labels_copy.start()
    left_copy = pltpu.make_async_copy(left_ref, left_v, local_sem.at[0])
    left_copy.start()
    bits_copy = pltpu.make_async_copy(bits_ref, bits_i, local_sem.at[4])
    bits_copy.start()
    own_t0 = pltpu.make_async_copy(tens_ref.at[0, :, pl.ds(0, half)], t0, local_sem.at[1])
    own_t1 = pltpu.make_async_copy(
        tens_ref.at[0, :, pl.ds(half, half)], t1.at[:, pl.ds(0, half)], local_sem.at[1]
    )

    @pl.when(sect == 0)
    def _():
        own_t0.start()

    @pl.when(sect == 1)
    def _():
        own_t1.start()

    barrier = pltpu.get_barrier_semaphore()

    far_first = sorted(range(1, ranks), key=lambda k: abs(k - ranks // 2))

    pl.semaphore_signal(barrier, inc=1, device_id=(1 - sect, blk), device_id_type=MESH)
    for k in far_first:
        pl.semaphore_signal(
            barrier, inc=1, device_id=(sect, lax.rem(blk + k, ranks)), device_id_type=MESH
        )

    labels_copy.wait()
    labels = jnp.broadcast_to(labels_v[...].reshape(1, count_blocks), (count_blocks, count_blocks))
    place = lax.broadcasted_iota(jnp.int32, (count_blocks, count_blocks), 0)
    charge = lax.broadcasted_iota(jnp.int32, (count_blocks, count_blocks), 1)
    inv_v[...] = jnp.max(jnp.where(labels.T == charge, place, 0), axis=0, keepdims=True)
    inv_copy = pltpu.make_async_copy(inv_v, inv_s, local_sem.at[2])
    inv_copy.start()
    left_copy.wait()

    def stage(step, carry):
        for u in range(8):
            i = step * 8 + u
            left_b[i] = left_v[:, pl.ds(pl.multiple_of(i * block, block), block)]
        return carry

    lax.fori_loop(0, count_blocks // 8, stage, 0)
    bits_v[...] = jnp.zeros_like(bits_v)
    bits_copy.wait()
    bits_v[0:1, 0:rows] = bits_i[...].astype(jnp.float32)
    pl.semaphore_wait(barrier, ranks)

    pieces0 = [(h, min(2, half - h)) for h in range(0, half, 2)]
    pieces1 = [(j, min(2, half + 1 - j)) for j in range(0, half + 1, 2)]

    def tens_to_one(i):
        first, many = pieces0[i]
        return pltpu.make_async_remote_copy(
            src_ref=tens_ref.at[0, :, pl.ds(half + first, many)],
            dst_ref=t0.at[:, pl.ds(first, many)],
            send_sem=t0_send.at[i],
            recv_sem=t0_recv.at[i],
            device_id=(1, blk),
            device_id_type=MESH,
        )

    def tens_to_zero(i):
        first, many = pieces1[i]
        return pltpu.make_async_remote_copy(
            src_ref=tens_ref.at[0, :, pl.ds(first, many)],
            dst_ref=t1.at[:, pl.ds(first, many)],
            send_sem=t1_send.at[i],
            recv_sem=t1_recv.at[i],
            device_id=(0, blk),
            device_id_type=MESH,
        )

    def send_piece(i):
        if i < len(pieces0):

            @pl.when(sect == 0)
            def _():
                tens_to_one(i).start()

        @pl.when(sect == 1)
        def _():
            tens_to_zero(i).start()

    tens_back = pltpu.make_async_remote_copy(
        src_ref=tens_ref.at[0, :, pl.ds(0, 1)],
        dst_ref=t1.at[:, pl.ds(half, 1)],
        send_sem=t1_send.at[half + 1],
        recv_sem=t1_recv.at[half + 1],
        device_id=(1, lax.rem(blk + ranks - 1, ranks)),
        device_id_type=MESH,
    )

    send_piece(0)
    inv_copy.wait()

    def order(b, carry):
        for h in range(half):
            where = inv_s[0, group * b + half * sect + h]
            ordered[b, :, h * block : (h + 1) * block] = left_b[where]
        return carry

    lax.fori_loop(0, ranks, order, 0)

    mine = pl.ds(pl.multiple_of(blk * rows, rows), rows)

    def send_left(k):
        other = lax.rem(blk + k, ranks)
        pltpu.make_async_remote_copy(
            src_ref=ordered.at[other],
            dst_ref=state.at[mine],
            send_sem=left_sem.at[0],
            recv_sem=left_sem.at[1],
            device_id=(sect, other),
            device_id_type=MESH,
        ).start()

    for i, k in enumerate(far_first):
        send_left(k)
        if i % 3 == 2 and 0 < i // 3 + 1 < len(pieces1):
            send_piece(i // 3 + 1)

    @pl.when(sect == 1)
    def _():
        tens_back.start()

    state[mine, :] = ordered[blk]

    others = state.at[pl.ds(0, (ranks - 1) * rows)]
    pltpu.make_async_copy(others, others, left_sem.at[1]).wait()

    @pl.when(sect == 0)
    def _():
        own_t0.wait()

    sums[...] = jnp.zeros_like(sums)

    def site_zero(h, carry):
        for i, (first, _) in enumerate(pieces0):

            @pl.when((sect == 1) & (h == first))
            def _():
                tens_to_one(i).wait_recv()

        both = jnp.concatenate([t0[0, h], t0[1, h]], axis=1)
        image = jnp.dot(
            state[:, pl.ds(pl.multiple_of(h * block, block), block)],
            both,
            preferred_element_type=jnp.float32,
        )
        images[h] = image
        stay, raised = image[:, :block], image[:, block:]
        sums[0] += stay * stay
        sums[1] += raised * raised
        return carry

    lax.fori_loop(0, half, site_zero, 0)
    norm_stay = jnp.sum(sums[0], axis=1, keepdims=True)
    norm_raised = jnp.sum(sums[1], axis=1, keepdims=True)

    lane = lax.broadcasted_iota(jnp.int32, (samples, block), 1)
    row = lax.broadcasted_iota(jnp.int32, (samples, block), 0)

    def fill(part, columns):
        spread = jnp.zeros((samples, block), jnp.float32)
        for v, column in enumerate(columns):
            spread = jnp.where(lane // rows == v, column, spread)
        spread = jnp.where(lane % rows == row % rows, spread, 0.0)
        for b in range(ranks):
            part[b] = jnp.sum(spread[b * rows : (b + 1) * rows], axis=0, keepdims=True)

    def send_part(part, target):
        def one(k):
            rank = lax.rem(blk + k, ranks)
            slot = lax.rem(target * ranks + rank - me + total, total) - 1
            pltpu.make_async_remote_copy(
                src_ref=part.at[rank],
                dst_ref=inbox.at[slot],
                send_sem=part_sem.at[0],
                recv_sem=part_sem.at[1],
                device_id=(target, rank),
                device_id_type=MESH,
            ).start()

        for k in far_first:
            one(k)

        @pl.when(sect != target)
        def _():
            one(0)

    fill(part0, [norm_stay, norm_raised])
    send_part(part0, 0)

    scales = [lax.rsqrt(norm_stay / part_width + EPS), lax.rsqrt(norm_raised / part_width + EPS)]

    def halves(value):
        high = value.astype(jnp.bfloat16)
        low = (value - high.astype(jnp.float32)).astype(jnp.bfloat16)
        return jnp.concatenate([high, low], axis=1)

    @pl.when(sect == 1)
    def _():
        own_t1.wait()

    def site_one(h, carry):
        for i, (first, _) in enumerate(pieces1):

            @pl.when((sect == 0) & (h == max(first - 1, 0)))
            def _():
                tens_to_zero(i).wait_recv()

        @pl.when((sect == 1) & (h == half - 1))
        def _():
            tens_back.wait_recv()

        for first in range(2):
            both = jnp.concatenate([t1[0, h + first], t1[1, h + first]], axis=1)
            value = images[h, :, first * block : (first + 1) * block] * scales[first]
            image = jnp.dot(
                halves(value),
                jnp.concatenate([both, both], axis=0),
                preferred_element_type=jnp.float32,
            )
            for second in range(2):
                piece = image[:, second * block : (second + 1) * block]
                sums[2 + 2 * second + first] += piece * piece
        return carry

    lax.fori_loop(0, half, site_one, 0)
    columns = [norm_stay, norm_raised]
    for v in range(2, 6):
        columns.append(jnp.sum(sums[v], axis=1, keepdims=True))
    fill(part1, columns)
    own_bits = pltpu.roll(bits_v[...], 6 * rows, 1)[0:1]
    part1[blk] = part1[blk] + jnp.where(sect == 0, own_bits, 0.0)
    send_part(part1, 1)

    pltpu.make_async_copy(inbox, inbox, part_sem.at[1]).wait()
    stack[0:1, :] = jnp.where(sect == 0, part0[blk], part1[blk])
    for k in range(total - 1):
        stack[k + 1 : k + 2, :] = inbox[k]
    all_parts = stack[...]
    sums_all = jnp.sum(all_parts, axis=0, keepdims=True)
    here = bits_v[...] == 1.0

    def value(source, v):
        wide = jnp.broadcast_to(source, (8, block))
        return wide if v == 0 else pltpu.roll(wide, block - v * rows, 1)

    norm_zero, norm_one = value(sums_all, 0), value(sums_all, 1)

    @pl.when(sect == 0)
    def _():
        prob = jnp.where(here, norm_one, norm_zero) / (norm_zero + norm_one)
        out_ref[0:1, :] = prob[0:1]
        out_ref[1:2, :] = jnp.log(prob)[0:1]

    @pl.when(sect == 1)
    def _():
        weight = (all_parts / part_width + EPS) / (sums_all / width + EPS)
        where = lax.broadcasted_iota(jnp.int32, (total, block), 1)
        weight = jnp.where(
            where < 4 * rows, pltpu.roll(weight, 2 * rows, 1), pltpu.roll(weight, 4 * rows, 1)
        )
        later = jnp.sum(all_parts * weight, axis=0, keepdims=True)
        before = value(sums_all, 6) == 1.0
        prob0 = jnp.where(before, norm_one, norm_zero) / (norm_zero + norm_one)
        zero = jnp.where(before, value(later, 3), value(later, 2))
        one = jnp.where(before, value(later, 5), value(later, 4))
        prob = jnp.where(here, one, zero) / (zero + one)
        out_ref[0:1, :] = prob[0:1]
        out_ref[1:2, :] = (jnp.log(prob0) + jnp.log(prob))[0:1]

    pltpu.make_async_copy(others, others, left_sem.at[0]).wait()
    pltpu.make_async_copy(inbox, inbox, part_sem.at[0]).wait()

    @pl.when(sect == 0)
    def _():
        for i in range(len(pieces0)):
            tens_to_one(i).wait_send()

    @pl.when(sect == 1)
    def _():
        for i in range(len(pieces1)):
            tens_to_zero(i).wait_send()
        tens_back.wait_send()


def body_pair(ranks, bits, labels, left, tensors):
    rows = bits.shape[1]
    count_blocks = labels.shape[0]
    block = tensors.shape[-1]
    group = tensors.shape[2]
    half = group // 2
    vmem = pl.BlockSpec(memory_space=pltpu.VMEM)
    hbm = pl.BlockSpec(memory_space=pl.ANY)
    dma = pltpu.SemaphoreType.DMA
    scored = pl.pallas_call(
        functools.partial(pair_kernel, ranks),
        out_shape=pltpu.VMEM((2, block), jnp.float32),
        in_specs=[hbm, hbm, hbm, hbm],
        out_specs=vmem,
        scratch_shapes=[
            pltpu.VMEM(bits.shape, jnp.int32),
            pltpu.VMEM(labels.shape, jnp.int32),
            pltpu.VMEM(left.shape, jnp.bfloat16),
            pltpu.VMEM((count_blocks, rows, block), jnp.bfloat16),
            pltpu.VMEM((1, count_blocks), jnp.int32),
            pltpu.SMEM((1, count_blocks), jnp.int32),
            pltpu.VMEM((ranks, rows, half * block), jnp.bfloat16),
            pltpu.VMEM((ranks * rows, half * block), jnp.bfloat16),
            pltpu.VMEM((half, ranks * rows, 2 * block), jnp.float32),
            pltpu.VMEM((6, ranks * rows, block), jnp.float32),
            pltpu.VMEM((2, half, block, block), jnp.bfloat16),
            pltpu.VMEM((2, half + 1, block, block), jnp.bfloat16),
            pltpu.VMEM((ranks, 1, block), jnp.float32),
            pltpu.VMEM((ranks, 1, block), jnp.float32),
            pltpu.VMEM((2 * ranks - 1, 1, block), jnp.float32),
            pltpu.VMEM((2 * ranks, block), jnp.float32),
            pltpu.VMEM((8, block), jnp.float32),
            dma((5,)),
            dma((half,)),
            dma((half,)),
            dma((half + 2,)),
            dma((half + 2,)),
            dma((2,)),
            dma((2,)),
        ],
        compiler_params=pltpu.CompilerParams(
            collective_id=0, has_side_effects=True, vmem_limit_bytes=60 * 1024 * 1024
        ),
        name="score_pair",
    )(bits, labels, left, tensors)
    return scored[0:1, :rows], scored[1:2, :rows]


def solution(mesh):
    in_specs = (P("sect", "blk"), P(), P("blk", None), P("sect", None, "blk", None, None))
    out_specs = (P("sect", "blk"), P("sect", "blk"))
    if mesh.shape["sect"] == 2:
        body = functools.partial(body_pair, mesh.shape["blk"])
    else:
        body = body_many
    return jax.shard_map(body, mesh=mesh, in_specs=in_specs, out_specs=out_specs, check_vma=False)
```
